32 devices in a mesh: dp: 8 (over y, x, core), fsdp: 4 (over z).
Axes of the slice: x: 2, y: 2, z: 4, core: 2. Of those that a mesh axis runs over, the one named last changes fastest.
Arguments:
- tokens: bfloat16 [36864, 384], P(('dp', 'fsdp')), may hold values from -6 to 6
- cotangent: bfloat16 [36864, 384], P(('dp', 'fsdp')), may hold values from -6 to 6
- rel_index: int32 [144, 144], replicated, may hold values from 0 to 3311
- qkv_weight: float32 [384, 1152], P('fsdp'), may hold values from -0.3125 to 0.3125
- proj_weight: float32 [384, 384], P('fsdp'), may hold values from -1.75 to 1.75
- fc1_weight: float32 [384, 1536], P('fsdp'), may hold values from -0.3125 to 0.3125
- fc2_weight: float32 [1536, 384], P('fsdp'), may hold values from -0.15625 to 0.15625
- qkv_momentum: float32 [384, 1152], P('fsdp'), may hold values from -5 to 5
- proj_momentum: float32 [384, 384], P('fsdp'), may hold values from -1.25 to 1.25
- fc1_momentum: float32 [384, 1536], P('fsdp'), may hold values from -3.5 to 3.5
- fc2_momentum: float32 [1536, 384], P('fsdp'), may hold values from -3.5 to 3.5
- qkv_left: float32 [384, 384], P('fsdp')
- qkv_right: float32 [1152, 1152], P('fsdp')
- proj_left: float32 [384, 384], P('fsdp')
- proj_right: float32 [384, 384], P('fsdp')
- fc1_left: float32 [384, 384], P('fsdp')
- fc1_right: float32 [1536, 1536], P('fsdp')
- fc2_left: float32 [1536, 1536], P('fsdp')
- fc2_right: float32 [384, 384], P('fsdp')
- qkv_left_root: float32 [384, 384], P('fsdp')
- qkv_right_root: float32 [1152, 1152], P('fsdp'), as said below
- proj_left_root: float32 [384, 384], P('fsdp')
- proj_right_root: float32 [384, 384], P('fsdp'), as said below
- fc1_left_root: float32 [384, 384], P('fsdp')
- fc1_right_root: float32 [1536, 1536], P('fsdp'), as said below
- fc2_left_root: float32 [1536, 1536], P('fsdp')
- fc2_right_root: float32 [384, 384], P('fsdp'), as said below
- norm_gains: float32 [768], replicated, may hold values from 0.5 to 1.5
- biases: float32 [3072], replicated, may hold values from -1.25 to 1.25
- bias_table: float32 [8, 12, 3312], replicated, may hold values from -3 to 3
- gains_first: float32 [768], replicated, may hold values from -0.625 to 0.625
- gains_second: float32 [768], replicated, may hold values from 0.001 to 0.004
- biases_first: float32 [3072], replicated, may hold values from -0.625 to 0.625
- biases_second: float32 [3072], replicated, may hold values from 0.001 to 0.004
- table_first: float32 [8, 12, 3312], replicated, may hold values from -0.015625 to 0.015625
- table_second: float32 [8, 12, 3312], replicated, may hold values from 5e-07 to 2e-06
Outputs:
- block_output: bfloat16 [36864, 384], P(('dp', 'fsdp'))
- input_grad: bfloat16 [36864, 384], P(('dp', 'fsdp'))
- qkv_weight_new: float32 [384, 1152], P('fsdp')
- proj_weight_new: float32 [384, 384], P('fsdp')
- fc1_weight_new: float32 [384, 1536], P('fsdp')
- fc2_weight_new: float32 [1536, 384], P('fsdp')
- qkv_momentum_new: float32 [384, 1152], P('fsdp')
- proj_momentum_new: float32 [384, 384], P('fsdp')
- fc1_momentum_new: float32 [384, 1536], P('fsdp')
- fc2_momentum_new: float32 [1536, 384], P('fsdp')
- qkv_left_new: float32 [384, 384], P('fsdp')
- qkv_right_new: float32 [1152, 1152], P('fsdp')
- proj_left_new: float32 [384, 384], P('fsdp')
- proj_right_new: float32 [384, 384], P('fsdp')
- fc1_left_new: float32 [384, 384], P('fsdp')
- fc1_right_new: float32 [1536, 1536], P('fsdp')
- fc2_left_new: float32 [1536, 1536], P('fsdp')
- fc2_right_new: float32 [384, 384], P('fsdp')
- gains_new: float32 [768], replicated
- biases_new: float32 [3072], replicated
- table_new: float32 [8, 12, 3312], replicated
- gains_first_new: float32 [768], replicated
- biases_first_new: float32 [3072], replicated
- table_first_new: float32 [8, 12, 3312], replicated
- gains_second_new: float32 [768], replicated
- biases_second_new: float32 [3072], replicated
- table_second_new: float32 [8, 12, 3312], replicated
The draws below stay inside these ranges and needn't reach their ends.
Inputs may be any that keep to these rules, and one draw needn't show every extreme that they name: qkv_right_root is symmetric. proj_right_root is symmetric. fc1_right_root is symmetric. fc2_right_root is symmetric.
All inputs are finite; a program needn't handle non-finite values.
Results may differ from the reference program's by a relative error of at most 0.012.
Values may be sent and summed in bfloat16 or wider, within the bound.
No kernel may reach another device: no remote copies, remote signals or barrier semaphores. Data moves between devices by JAX's collectives and lax.ppermute only.
A program may use at most 256 MiB of HBM per device.

```python
import math
import jax
import jax.numpy as jnp
from jax import lax

D = 384
HEADS = 12
HEAD = 32
FF = 1536
NTYPE = 8
STEP = 5
WTOK = 144
NREL = 3312
BIAS_LEN = 3072
TOKENS = 36864


def diagonal_draw(key, matrix_order, base_level):
    entries = jax.random.uniform(key, (matrix_order,), jnp.float32, math.log(base_level), math.log(4.0 * base_level))
    return jnp.diag(jnp.exp(entries))


def root_draw(key, matrix_order):
    diag_key, rest_key = jax.random.split(key)
    entries = jnp.exp(jax.random.uniform(diag_key, (matrix_order,), jnp.float32, 0.0, math.log(4.0)))
    noise_table = jax.random.uniform(rest_key, (matrix_order, matrix_order), jnp.float32, -1.0, 1.0)
    return jnp.diag(entries) + (noise_table + noise_table.T) * (0.75 / math.sqrt(matrix_order))


def draw_qkv_left(key, part):
    key = jax.random.fold_in(key, 11)
    return diagonal_draw(key, D, 0.64)


def draw_qkv_right(key, part):
    key = jax.random.fold_in(key, 12)
    return diagonal_draw(key, 3 * D, 0.64)


def draw_proj_left(key, part):
    key = jax.random.fold_in(key, 13)
    return diagonal_draw(key, D, 0.04)


def draw_proj_right(key, part):
    key = jax.random.fold_in(key, 14)
    return diagonal_draw(key, D, 0.04)


def draw_fc1_left(key, part):
    key = jax.random.fold_in(key, 15)
    return diagonal_draw(key, D, 0.36)


def draw_fc1_right(key, part):
    key = jax.random.fold_in(key, 16)
    return diagonal_draw(key, FF, 0.36)


def draw_fc2_left(key, part):
    key = jax.random.fold_in(key, 17)
    return diagonal_draw(key, FF, 0.36)


def draw_fc2_right(key, part):
    key = jax.random.fold_in(key, 18)
    return diagonal_draw(key, D, 0.36)


def draw_qkv_left_root(key, part):
    key = jax.random.fold_in(key, 21)
    return root_draw(key, D)


def draw_qkv_right_root(key, part):
    key = jax.random.fold_in(key, 22)
    return root_draw(key, 3 * D)


def draw_proj_left_root(key, part):
    key = jax.random.fold_in(key, 23)
    return root_draw(key, D)


def draw_proj_right_root(key, part):
    key = jax.random.fold_in(key, 24)
    return root_draw(key, D)


def draw_fc1_left_root(key, part):
    key = jax.random.fold_in(key, 25)
    return root_draw(key, D)


def draw_fc1_right_root(key, part):
    key = jax.random.fold_in(key, 26)
    return root_draw(key, FF)


def draw_fc2_left_root(key, part):
    key = jax.random.fold_in(key, 27)
    return root_draw(key, FF)


def draw_fc2_right_root(key, part):
    key = jax.random.fold_in(key, 28)
    return root_draw(key, D)


def place_ends(drawn, key, low, top_value):
    spot = [jax.random.randint(jax.random.fold_in(key, axis), (), 0, length) for axis, length in enumerate(drawn.shape)]
    widest = drawn.shape.index(max(drawn.shape))
    next_to = spot[:widest] + [(spot[widest] + 1) % drawn.shape[widest]] + spot[widest + 1:]
    return drawn.at[tuple(spot)].set(low).at[tuple(next_to)].set(top_value)


def block_levels(stream_key, shape, shards, smallest, high):
    gain = 1.0
    for position, shards_of in shards:
        heights = jax.random.uniform(jax.random.fold_in(jax.random.fold_in(stream_key, 6), position), (shards_of,), jnp.float32, smallest / len(shards), high / len(shards))
        gain = gain * jnp.repeat(jnp.exp(heights), shape[position] // shards_of).reshape((-1,) + (1,) * (len(shape) - 1 - position))
    return gain


def noise(key, extent, scale, bound, pieces=(), held_as=jnp.bfloat16):
    values = scale * jax.random.normal(key, extent, jnp.float32)
    if pieces:
        values = values * block_levels(key, extent, pieces, -0.22, 0.18)
    return jnp.clip(values, -bound, bound).astype(held_as)


def setup_inputs(seed: int = 0) -> dict:
    key_of = jax.random.split(jax.random.key(seed), 37)
    tokens = noise(key_of[0], (TOKENS, D), 1.0, 6.0, ((0, 32),))
    cotangent = noise(key_of[1], (TOKENS, D), 1.0, 6.0, ((0, 32),))
    rel_index = place_ends(jax.random.randint(key_of[2], (WTOK, WTOK), 0, NREL), jax.random.fold_in(key_of[2], 1), 0, NREL - 1).astype(jnp.int32)
    qkv_weight = noise(key_of[3], (D, 3 * D), D ** -0.5, 0.3125, ((0, 4),), jnp.float32)
    proj_weight = noise(key_of[4], (D, D), (D // 32) ** -0.5, 1.75, ((0, 4),), jnp.float32)
    fc1_weight = noise(key_of[5], (D, FF), D ** -0.5, 0.3125, ((0, 4),), jnp.float32)
    fc2_weight = noise(key_of[6], (FF, D), FF ** -0.5, 0.15625, ((0, 4),), jnp.float32)
    qkv_momentum = noise(key_of[7], (D, 3 * D), 0.8, 5.0, ((0, 4),), jnp.float32)
    proj_momentum = noise(key_of[8], (D, D), 0.2, 1.25, ((0, 4),), jnp.float32)
    fc1_momentum = noise(key_of[9], (D, FF), 0.6, 3.5, ((0, 4),), jnp.float32)
    fc2_momentum = noise(key_of[10], (FF, D), 0.6, 3.5, ((0, 4),), jnp.float32)
    qkv_left = draw_qkv_left(jax.random.fold_in(key_of[36], 71), 0)
    qkv_right = draw_qkv_right(jax.random.fold_in(key_of[36], 71), 0)
    proj_left = draw_proj_left(jax.random.fold_in(key_of[36], 71), 0)
    proj_right = draw_proj_right(jax.random.fold_in(key_of[36], 71), 0)
    fc1_left = draw_fc1_left(jax.random.fold_in(key_of[36], 71), 0)
    fc1_right = draw_fc1_right(jax.random.fold_in(key_of[36], 71), 0)
    fc2_left = draw_fc2_left(jax.random.fold_in(key_of[36], 71), 0)
    fc2_right = draw_fc2_right(jax.random.fold_in(key_of[36], 71), 0)
    qkv_left_root = draw_qkv_left_root(jax.random.fold_in(key_of[36], 71), 0)
    qkv_right_root = draw_qkv_right_root(jax.random.fold_in(key_of[36], 71), 0)
    proj_left_root = draw_proj_left_root(jax.random.fold_in(key_of[36], 71), 0)
    proj_right_root = draw_proj_right_root(jax.random.fold_in(key_of[36], 71), 0)
    fc1_left_root = draw_fc1_left_root(jax.random.fold_in(key_of[36], 71), 0)
    fc1_right_root = draw_fc1_right_root(jax.random.fold_in(key_of[36], 71), 0)
    fc2_left_root = draw_fc2_left_root(jax.random.fold_in(key_of[36], 71), 0)
    fc2_right_root = draw_fc2_right_root(jax.random.fold_in(key_of[36], 71), 0)
    norm_gains = jnp.clip(1.0 + 0.1 * jax.random.normal(key_of[27], (2 * D,), jnp.float32), 0.5, 1.5)
    biases = noise(key_of[28], (BIAS_LEN,), 0.2, 1.25, (), jnp.float32)
    bias_table = noise(key_of[29], (NTYPE, HEADS, NREL), 0.5, 3.0, (), jnp.float32)
    gains_first = noise(key_of[30], (2 * D,), 0.11, 0.625, (), jnp.float32)
    gains_second = jnp.clip(jnp.exp(jax.random.uniform(key_of[31], (2 * D,), jnp.float32, math.log(0.001), math.log(0.004))), 0.001, 0.004)
    biases_first = noise(key_of[32], (BIAS_LEN,), 0.11, 0.625, (), jnp.float32)
    biases_second = jnp.clip(jnp.exp(jax.random.uniform(key_of[33], (BIAS_LEN,), jnp.float32, math.log(0.001), math.log(0.004))), 0.001, 0.004)
    table_first = noise(key_of[34], (NTYPE, HEADS, NREL), 0.0025, 0.015625, (), jnp.float32)
    table_second = jnp.clip(jnp.exp(jax.random.uniform(key_of[35], (NTYPE, HEADS, NREL), jnp.float32, math.log(4.999999987376214e-07), math.log(1.9999999949504854e-06))), 4.999999987376214e-07, 1.9999999949504854e-06)
    return dict(tokens=tokens, cotangent=cotangent, rel_index=rel_index, qkv_weight=qkv_weight, proj_weight=proj_weight, fc1_weight=fc1_weight, fc2_weight=fc2_weight, qkv_momentum=qkv_momentum, proj_momentum=proj_momentum, fc1_momentum=fc1_momentum, fc2_momentum=fc2_momentum, qkv_left=qkv_left, qkv_right=qkv_right, proj_left=proj_left, proj_right=proj_right, fc1_left=fc1_left, fc1_right=fc1_right, fc2_left=fc2_left, fc2_right=fc2_right, qkv_left_root=qkv_left_root, qkv_right_root=qkv_right_root, proj_left_root=proj_left_root, proj_right_root=proj_right_root, fc1_left_root=fc1_left_root, fc1_right_root=fc1_right_root, fc2_left_root=fc2_left_root, fc2_right_root=fc2_right_root, norm_gains=norm_gains, biases=biases, bias_table=bias_table, gains_first=gains_first, gains_second=gains_second, biases_first=biases_first, biases_second=biases_second, table_first=table_first, table_second=table_second)


@jax.custom_vjp
def low(v):
    return lax.optimization_barrier(v.astype(jnp.bfloat16)).astype(jnp.float32)

@jax.custom_vjp
def low_back(v):
    return v

def low_keep(v):
    return (low(v), None)

def low_pass(kept, grad):
    return (grad,)

def back_keep(v):
    return (v, None)

def back_low(kept, grad):
    return (low(grad),)
low.defvjp(low_keep, low_pass)
low_back.defvjp(back_keep, back_low)
norm_eps = 1e-05
adam_first = 0.9
adam_second = 0.999
adam_eps = 1e-08
adam_rate = 0.3
shampoo_decay = 0.5
shampoo_momentum = 0.9
matrix_rates = (0.02, 0.1, 0.02, 0.02)
highest = lax.Precision.HIGHEST

def layer_norm(values, scales, offset):
    centre = values - lax.optimization_barrier(jnp.mean(values, axis=-1, keepdims=True))
    spread = lax.optimization_barrier(jnp.mean(centre * centre, axis=-1, keepdims=True))
    return centre * lax.rsqrt(spread + norm_eps) * scales + offset

def matmul(former, latter):
    return jnp.dot(former, latter, precision=highest, preferred_element_type=jnp.float32)

def window_block(params, window_rows, window_kinds, rel_index):
    qkv_weight, proj_weight, fc1_weight, fc2_weight, norm_gains, biases, bias_table = params
    model_width = qkv_weight.shape[0]
    window_count = window_rows.shape[0] // WTOK
    normed_one = low(layer_norm(window_rows, norm_gains[:model_width], biases[:model_width]))
    packed = low(low_back(matmul(normed_one, low(qkv_weight))))
    packed = packed.reshape(window_count, WTOK, 3, HEADS, HEAD)
    scores = jnp.einsum('wqhc,wkhc->whqk', packed[:, :, 0], packed[:, :, 1], precision=highest) * HEAD ** (-0.5)
    offsets = bias_table[window_kinds][:, :, rel_index]
    scores = low_back(scores + offsets)
    row_top = lax.optimization_barrier(jnp.max(scores, axis=-1, keepdims=True))
    weights = jnp.exp(scores - row_top)
    attention = low(weights / lax.optimization_barrier(jnp.sum(weights, axis=-1, keepdims=True)))
    mixed_heads = jnp.einsum('whqk,wkhc->wqhc', attention, packed[:, :, 2], precision=highest)
    mixed_heads = low(low_back(mixed_heads.reshape(window_count * WTOK, model_width)))
    attended = low_back(matmul(mixed_heads, low(proj_weight)) + biases[2 * model_width:3 * model_width])
    middle = window_rows + attended
    normed_two = low(layer_norm(middle, norm_gains[model_width:], biases[model_width:2 * model_width]))
    hidden = low_back(matmul(normed_two, low(fc1_weight)) + biases[4 * model_width:])
    activated = low(jax.nn.gelu(hidden))
    branch = low_back(matmul(activated, low(fc2_weight)) + biases[3 * model_width:4 * model_width])
    return middle + branch

def shampoo(weight, momentum, left_stat, right_stat, left_root, right_root, gradient, step_rate):
    new_left = shampoo_decay * left_stat + (1.0 - shampoo_decay) * matmul(gradient, gradient.T) / gradient.shape[1]
    new_right = shampoo_decay * right_stat + (1.0 - shampoo_decay) * matmul(gradient.T, gradient) / gradient.shape[0]
    new_momentum = shampoo_momentum * momentum + matmul(left_root, matmul(gradient, right_root))
    return (weight - step_rate * new_momentum, new_momentum, new_left, new_right)

def adam_update(parameter, first_moment, second_moment, gradient):
    new_first = adam_first * first_moment + (1.0 - adam_first) * gradient
    new_second = adam_second * second_moment + (1.0 - adam_second) * gradient * gradient
    first_hat = new_first / (1.0 - adam_first ** STEP)
    second_hat = new_second / (1.0 - adam_second ** STEP)
    return (parameter - adam_rate * first_hat / (jnp.sqrt(second_hat) + adam_eps), new_first, new_second)

def reference(tokens, cotangent, rel_index, qkv_weight, proj_weight, fc1_weight, fc2_weight, qkv_momentum, proj_momentum, fc1_momentum, fc2_momentum, qkv_left, qkv_right, proj_left, proj_right, fc1_left, fc1_right, fc2_left, fc2_right, qkv_left_root, qkv_right_root, proj_left_root, proj_right_root, fc1_left_root, fc1_right_root, fc2_left_root, fc2_right_root, norm_gains, biases, bias_table, gains_first, gains_second, biases_first, biases_second, table_first, table_second):
    windows = TOKENS // WTOK
    group_size = max((candidate for candidate in range(1, 29) if windows % candidate == 0))
    blocks = windows // group_size
    inputs = tokens.astype(jnp.float32).reshape(blocks, group_size * WTOK, D)
    window_kinds = (jnp.arange(windows, dtype=jnp.int32) % NTYPE).reshape(blocks, group_size)
    params = (qkv_weight, proj_weight, fc1_weight, fc2_weight, norm_gains, biases, bias_table)

    def forward(params, inputs):

        def one_block(operands):
            return window_block(params, operands[0], operands[1], rel_index)
        return lax.map(jax.checkpoint(one_block), (inputs, window_kinds))
    outputs, pullback = jax.vjp(forward, params, inputs)
    gradients, d_inputs = pullback(cotangent.astype(jnp.float32).reshape(inputs.shape))
    scaled = [gradient / math.sqrt(TOKENS) for gradient in gradients]
    qkv_out = shampoo(qkv_weight, qkv_momentum, qkv_left, qkv_right, qkv_left_root, qkv_right_root, scaled[0], matrix_rates[0])
    proj_out = shampoo(proj_weight, proj_momentum, proj_left, proj_right, proj_left_root, proj_right_root, scaled[1], matrix_rates[1])
    fc1_out = shampoo(fc1_weight, fc1_momentum, fc1_left, fc1_right, fc1_left_root, fc1_right_root, scaled[2], matrix_rates[2])
    fc2_out = shampoo(fc2_weight, fc2_momentum, fc2_left, fc2_right, fc2_left_root, fc2_right_root, scaled[3], matrix_rates[3])
    gains_out = adam_update(norm_gains, gains_first, gains_second, scaled[4])
    biases_out = adam_update(biases, biases_first, biases_second, scaled[5])
    table_out = adam_update(bias_table, table_first, table_second, scaled[6])
    block_output = outputs.reshape(TOKENS, D).astype(jnp.bfloat16)
    input_grad = d_inputs.reshape(TOKENS, D).astype(jnp.bfloat16)
    return (block_output, input_grad, qkv_out[0], proj_out[0], fc1_out[0], fc2_out[0], qkv_out[1], proj_out[1], fc1_out[1], fc2_out[1], qkv_out[2], qkv_out[3], proj_out[2], proj_out[3], fc1_out[2], fc1_out[3], fc2_out[2], fc2_out[3], gains_out[0], biases_out[0], table_out[0], gains_out[1], biases_out[1], table_out[1], gains_out[2], biases_out[2], table_out[2])
```

```python
import functools
import math

import jax
import jax.numpy as jnp
from jax import lax
from jax.experimental import pallas as pl
from jax.experimental.pallas import tpu as pltpu
from jax.sharding import PartitionSpec as P

HEADS = 12
HEAD = 32
STEP = 5
WTOK = 144
LANES = 128
GROUPS = HEADS // 4
SPAN = 5 * LANES
REST = WTOK - LANES
ROWBLOCKS = WTOK // 8
CHUNK = 384
LOG2E = 1.4426950408889634

norm_eps = 1e-05
adam_first = 0.9
adam_second = 0.999
adam_eps = 1e-08
adam_rate = 0.3
shampoo_decay = 0.5
shampoo_momentum = 0.9
matrix_rates = (0.02, 0.1, 0.02, 0.02)

F32 = jnp.float32
BF16 = jnp.bfloat16
I32 = jnp.int32


def dot_nn(a, b):
    return lax.dot_general(a, b, (((1,), (0,)), ((), ())), preferred_element_type=F32)


def dot_nt(a, b):
    return lax.dot_general(a, b, (((1,), (1,)), ((), ())), preferred_element_type=F32)


def dot_tn(a, b):
    return lax.dot_general(a, b, (((0,), (0,)), ((), ())), preferred_element_type=F32)


PACKED = 176
USED = 168
LOW = 256


def launch(body, ids, inputs, in_specs, outputs, out_specs, scratch, micros, grid=(1,), limit=32):
    micros = max(micros, 20) if micros > 3 else 3
    return pl.pallas_call(
        body,
        out_shape=tuple(
            pltpu.HBM(out[0], out[1]) if len(out) > 2 else jax.ShapeDtypeStruct(*out)
            for out in outputs
        ),
        grid_spec=pltpu.PrefetchScalarGridSpec(
            num_scalar_prefetch=1,
            grid=grid,
            in_specs=in_specs,
            out_specs=tuple(out_specs),
            scratch_shapes=scratch,
        ),
        compiler_params=pltpu.CompilerParams(vmem_limit_bytes=limit * 2**20),
        cost_estimate=pl.CostEstimate(
            flops=int(micros * 5e8), bytes_accessed=int(micros * 3e6), transcendentals=0
        ),
    )(ids, *inputs)


def far_away(*arrays):
    return [pltpu.with_memory_space_constraint(array, pltpu.HBM) for array in arrays]


def whole(shape):
    return pl.BlockSpec(tuple(shape), lambda *_: (0,) * len(shape))


def wholes(arrays):
    return [whole(array.shape) for array in arrays]


def ds(start, size, multiple=16):
    return pl.ds(pl.multiple_of(start, multiple), size)


def pack_kernel(ids, x, c, wq, wp, w1, w2, first, others, swapped):
    core = ids[0]
    half = first.shape[0]
    width = others.shape[1]
    here = ds(core * half, half)
    first[...] = wq[here, :].astype(BF16)
    others[0:half, :] = wp[here, :].astype(BF16)
    chunks = w1.shape[1] // width
    for i in range(chunks):
        others[half * (1 + i) : half * (2 + i), :] = w1[
            here, width * i : width * i + width
        ].astype(BF16)
    tall = w2.shape[0] // 2
    start = half * (1 + chunks)
    others[start : start + tall, :] = w2[ds(core * tall, tall), :].astype(BF16)
    rows = x.shape[0] // 2
    there = ds((1 - core) * rows, rows)
    swapped[0:rows, :] = x[there, :]
    swapped[rows : 2 * rows, :] = c[there, :]


def pack(ids, tokens, cotangent, wq, wp, w1, w2):
    piece, width = wp.shape
    half = piece // 2
    rows = half * (1 + w1.shape[1] // width) + w2.shape[0] // 2
    inputs = far_away(tokens, cotangent, wq, wp, w1, w2)
    outputs = (((half, wq.shape[1]), BF16), ((rows, width), BF16), (tokens.shape, BF16))
    return launch(
        pack_kernel, ids, inputs, wholes(inputs), outputs, [whole(o[0]) for o in outputs], [], 4
    )


def pack_roots_kernel(ids, bp, a1, b2, bq, b1, roots):
    core = ids[0]
    piece, width = bp.shape
    half = piece // 2
    here = ds(core * half, half)
    tall, side = b1.shape[0], b1.shape[1] // 2
    at = 0
    for i in range(side // width):
        cols = pl.ds(pl.multiple_of(core * side + width * i, LANES), width)
        roots[at : at + tall, :] = b1[:, cols].astype(BF16)
        at += tall
    for i, root in enumerate((bp, a1, b2)):
        roots[at + half * i : at + half * i + half, :] = root[here, :].astype(BF16)
    roots[at + 3 * half : at + tall // 2, :] = jnp.zeros((tall // 2 - 3 * half, width), BF16)
    at += tall // 2
    span = bq.shape[0] // 2
    for i in range(bq.shape[1] // width):
        roots[at : at + span, :] = bq[
            ds(core * span, span), width * i : width * i + width
        ].astype(BF16)
        at += span
    roots[at:, :] = jnp.zeros((roots.shape[0] - at, width), BF16)


def pack_roots(ids, bp, a1, b2, bq, b1):
    piece, width = bp.shape
    inputs = far_away(bp, a1, b2, bq, b1)
    tall = b1.shape[0]
    assert tall % 16 == 0 and 3 * piece <= tall
    lead = b1.size // 2 // width + tall // 2
    q_rows = bq.size // 2 // width
    while lead % q_rows or q_rows % 16:
        q_rows += 1
    out = ((lead + q_rows, width), BF16, "hbm")
    return launch(
        pack_roots_kernel, ids, inputs, wholes(inputs), (out,), (whole(out[0]),), [], 4
    )[0]


def bias_kernel(ids, rel_ref, table_ref, out_ref, idx_ref, square, wide, left, right, held):
    step = pl.program_id(0)
    heads, kinds, entries = table_ref.shape
    some = kinds // 2
    rows = some * heads
    highs = left.shape[0] // rows

    @pl.when(step == 0)
    def _():
        square[...] = jnp.zeros_like(square)
        square[0:WTOK, 0:WTOK] = rel_ref[...]
        turned = square[...].T
        idx_ref[0:WTOK, :] = turned[0:WTOK, 0:LANES]
        tail = turned[0:WTOK, LANES : 2 * LANES]
        for p in range(3):
            total = jnp.zeros((8, LANES), I32)
            for g in range(8):
                block = 8 * p + g
                if block < ROWBLOCKS:
                    piece = tail[8 * block : 8 * block + 8, :]
                    total = total + (pltpu.roll(piece, 16 * g, 1) if g else piece)
            idx_ref[WTOK + 8 * p : WTOK + 8 * p + 8, :] = total
        idx_ref[USED:PACKED, :] = jnp.zeros((PACKED - USED, LANES), I32)
        wide[...] = jnp.zeros_like(wide)
        for h in range(heads):
            mine = jnp.where(ids[0] == 0, table_ref[h, 0:some, :], table_ref[h, some:kinds, :])
            wide[some * h : some * h + some, 0:entries] = mine * LOG2E
        for b in range(highs):
            left[rows * b : rows * b + rows, :] = wide[:, LOW * b : LOW * b + LOW].astype(BF16)

    index = idx_ref[ds(step * 16, 16), :]
    low = (index & (LOW - 1)).astype(F32).astype(BF16)
    high = index // LOW
    place = lax.broadcasted_iota(I32, (LOW, LANES), 0).astype(F32).astype(BF16)
    one = jnp.ones((LOW, LANES), BF16)
    for k in range(16):
        right[:, LANES * k : LANES * k + LANES] = jnp.where(
            place == low[k : k + 1, :], one, jnp.zeros_like(one)
        )
    for k in range(0, 16, 2):
        found = dot_nn(left[...], right[:, LANES * k : LANES * k + 2 * LANES])
        for j in range(2):
            cols = slice(LANES * j, LANES * j + LANES)
            owner = high[k + j : k + j + 1, :]
            value = found[0:rows, cols]
            for b in range(1, highs):
                value = jnp.where(owner == b, found[rows * b : rows * b + rows, cols], value)
            held[pl.ds(k + j, rows, stride=16), :] = value
    out_ref[...] = held[...].reshape(rows, 16, LANES).astype(BF16)


def bias_gather(ids, rel_index, bias_table):
    heads, kinds, entries = bias_table.shape
    rows = kinds // 2 * heads
    highs = -(-entries // LOW)
    return launch(
        bias_kernel,
        ids,
        far_away(rel_index, bias_table),
        [
            whole(rel_index.shape),
            whole(bias_table.shape),
        ],
        (((rows, PACKED, LANES), BF16), ((PACKED, LANES), I32)),
        (pl.BlockSpec((rows, 16, LANES), lambda i, ids: (0, i, 0)), whole((PACKED, LANES))),
        [
            pltpu.VMEM((256, 256), I32),
            pltpu.VMEM((rows, highs * LOW), F32),
            pltpu.VMEM((highs * rows, LOW), BF16),
            pltpu.VMEM((LOW, 16 * LANES), BF16),
            pltpu.VMEM((rows * 16, LANES), F32),
        ],
        14,
        grid=(PACKED // 16,),
    )


def head_masks():
    lane = lax.broadcasted_iota(I32, (1, LANES), 1)
    return [(lane // HEAD == h).astype(F32).astype(BF16) for h in range(4)]


def spread(tile, masks):
    pieces = [tile[0:LANES] * masks[h] for h in range(4)]
    pieces += [tile[LANES:WTOK] * masks[h] for h in range(4)]
    pieces.append(jnp.zeros((64, LANES), BF16))
    return jnp.concatenate(pieces, axis=0)


def fold(turned):
    main = jnp.concatenate(
        [turned[HEAD * h : HEAD * h + HEAD, LANES * h : LANES * h + LANES] for h in range(4)],
        axis=0,
    ).T
    tail = turned[:, 4 * LANES : 5 * LANES]
    row = lax.broadcasted_iota(I32, tail.shape, 0) // HEAD
    place = lax.broadcasted_iota(I32, tail.shape, 1) // REST
    tail = jnp.where(row == place, tail, 0.0).T
    rest = tail[0:16] + tail[16:32] + tail[32:48] + tail[48:64]
    return jnp.concatenate([main, rest], axis=0)


def norm_stats(values):
    mean = jnp.mean(values, axis=-1, keepdims=True)
    centre = values - mean
    spread_of = jnp.mean(centre * centre, axis=-1, keepdims=True)
    rstd = lax.rsqrt(spread_of + norm_eps)
    return centre * rstd, rstd


def place_first(ids, near_ref, far_ref, full_ref):
    core, z = ids[0], ids[2]
    shards, half, _ = near_ref.shape
    for k in range(shards):
        base = (z ^ k) * (2 * half)
        full_ref[ds(base + core * half, half), :] = near_ref[k]
        full_ref[ds(base + (1 - core) * half, half), :] = far_ref[k]


def attend_kernel(
    ids,
    xn_ref,
    xf_ref,
    near_ref,
    far_ref,
    gain_ref,
    shift_ref,
    table_ref,
    qkv_ref,
    unit_ref,
    p_ref,
    o_ref,
    wq_ref,
    h1_ref,
):
    half, width = xn_ref.shape
    window = pl.program_id(0)

    @pl.when(window == 0)
    def _():
        place_first(ids, near_ref, far_ref, wq_ref)
        gain = gain_ref[0:1, 0:width]
        shift = shift_ref[0:1, 0:width]
        for which, ref in enumerate((xn_ref, xf_ref)):

            def norm_block(step, _):
                at = ds(step * WTOK + which * half, WTOK)
                unit, _ = norm_stats(ref[ds(step * WTOK, WTOK), :].astype(F32))
                unit_ref[at, :] = unit.astype(BF16)
                h1_ref[at, :] = (unit * gain + shift).astype(BF16)
                return 0

            lax.fori_loop(0, half // WTOK, norm_block, 0)
        for c in range(3):
            cols = slice(c * width, (c + 1) * width)
            qkv_ref[:, cols] = dot_nn(h1_ref[...], wq_ref[:, cols]).astype(BF16)

    at = ds(window * WTOK, WTOK)
    masks = head_masks()
    lane = lax.broadcasted_iota(I32, (8, LANES), 1) // REST
    for g in range(GROUPS):
        q4 = qkv_ref[at, LANES * g : LANES * g + LANES]
        k4 = qkv_ref[at, width + LANES * g : width + LANES * g + LANES]
        v4 = qkv_ref[at, 2 * width + LANES * g : 2 * width + LANES * g + LANES]
        raw = dot_nt(k4, spread(q4, masks))
        tails = [table_ref[4 * g + h, 0, WTOK:PACKED, :].astype(F32) for h in range(4)]
        pieces = []
        for block in range(ROWBLOCKS):
            p, slot = block // 8, block % 8
            total = jnp.zeros((8, LANES), F32)
            for h in range(4):
                piece = tails[h][8 * p : 8 * p + 8, :]
                turn = (16 * (h - slot)) % LANES
                if turn:
                    piece = pltpu.roll(piece, turn, 1)
                total = jnp.where(lane == h, piece, total)
            pieces.append(total)
        tail = jnp.concatenate(pieces, axis=0)
        for tile in range(5):
            cols = slice(LANES * tile, LANES * tile + LANES)
            offset = table_ref[4 * g + tile, 0, 0:WTOK, :].astype(F32) if tile < 4 else tail
            score = raw[:, cols] * (HEAD**-0.5 * LOG2E) + offset
            top = jnp.max(score, axis=0, keepdims=True)
            weight = jnp.exp2(score - top)
            total = jnp.sum(weight, axis=0, keepdims=True)
            p_ref[g, :, cols] = (weight * (1.0 / total)).astype(BF16)
        o_ref[:, LANES * g : LANES * g + LANES] = fold(dot_tn(v4, p_ref[g])).astype(BF16)


def own_half(array):
    return pl.BlockSpec((array.shape[0] // 2, array.shape[1]), lambda i, ids: (ids[0], 0))


def half_of(array, which):
    return pl.BlockSpec((array.shape[0] // 2, array.shape[1]), lambda i, ids: (which, 0))


def attend(ids, tokens, swapped, near, far, gains, shifts, table):
    rows, width = tokens.shape
    windows = rows // WTOK
    some = windows // 2
    (tokens,) = far_away(tokens)
    return launch(
        attend_kernel,
        ids,
        (
            tokens,
            swapped,
            near,
            far,
            gains,
            shifts,
            table.reshape(HEADS, some, PACKED, LANES),
        ),
        [
            own_half(tokens),
            half_of(swapped, 0),
            whole(near.shape),
            whole(far.shape),
            whole(gains.shape),
            whole(shifts.shape),
            pl.BlockSpec((HEADS, 1, PACKED, LANES), lambda i, ids: (0, i % some, 0, 0)),
        ],
        (
            ((rows, 3 * width), BF16, "hbm"),
            ((rows, width), BF16, "hbm"),
            ((windows * GROUPS, WTOK, SPAN), BF16, "hbm"),
            ((rows, width), BF16, "hbm"),
        ),
        (
            whole((rows, 3 * width)),
            whole((rows, width)),
            pl.BlockSpec((GROUPS, WTOK, SPAN), lambda i, ids: (i, 0, 0)),
            pl.BlockSpec((WTOK, width), lambda i, ids: (i, 0)),
        ),
        [pltpu.VMEM((width, 3 * width), BF16), pltpu.VMEM((rows, width), BF16)],
        3,
        grid=(windows,),
    )


def fold8(values):
    return jnp.sum(values.reshape(values.shape[0] // 8, 8, values.shape[1]), axis=0)


def put_rows(ref, start, row):
    for k in range(row.shape[1] // LANES):
        ref[start + k : start + k + 1, :] = row[:, LANES * k : LANES * k + LANES]


def middle_kernel(
    ids,
    x_hbm,
    swap_ref,
    o_hbm,
    c_hbm,
    near_hbm,
    far_hbm,
    gain_ref,
    bias_ref,
    outn_hbm,
    outf_hbm,
    dy_hbm,
    do_hbm,
    mine_hbm,
    theirs_hbm,
    small_ref,
    x_ref,
    o_ref,
    c_ref,
    pieces_ref,
    wp_ref,
    w1_ref,
    w2_ref,
    m_ref,
    h2_ref,
    h2t_ref,
    ct_ref,
    ot_ref,
    acc_ref,
    dh2_ref,
    u0_ref,
    u1_ref,
    da0_ref,
    da1_ref,
    a_ref,
    du_ref,
    g_ref,
    sem,
):
    core = ids[0]
    rows, width = o_ref.shape
    half = rows // 2
    ff = w1_ref.shape[1]
    part = u0_ref.shape[1]
    shards = near_hbm.shape[0]
    piece = width // shards
    used = []

    def start(source, target):
        copy = pltpu.make_async_copy(source, target, sem.at[len(used)])
        used.append(copy)
        copy.start()
        return copy

    own = ds(core * half, half)
    lead, tall = piece // 2, ff // shards // 2
    chunks = ff // width
    first = [
        start(near_hbm, pieces_ref.at[0]),
        start(far_hbm, pieces_ref.at[1]),
        start(o_hbm, o_ref),
        start(x_hbm.at[own], x_ref.at[0:half]),
        start(swap_ref.at[0:half], x_ref.at[half:rows]),
    ]
    second = [
        start(c_hbm.at[own], c_ref.at[0:half]),
        start(swap_ref.at[half:rows], c_ref.at[half:rows]),
    ]
    gain = gain_ref[0:1, width : 2 * width]
    shift = bias_ref[0:1, width : 2 * width]
    proj_bias = bias_ref[0:1, 2 * width : 3 * width]
    out_bias = bias_ref[0:1, 3 * width : 4 * width]
    small_ref[...] = jnp.zeros_like(small_ref)
    for copy in first:
        copy.wait()
    places = [
        (z, which, i) for z in range(shards) for i, which in enumerate((core, 1 - core))
    ]
    for z, which, i in places:
        wp_ref[ds(z * piece + which * lead, lead), :] = pieces_ref[i, z, 0:lead, :]
    for copy in second:
        copy.wait()

    def turn(source, target, k):
        cols = slice(LANES * k, LANES * k + LANES)
        target[:, cols] = source[cols, :].T

    line = 48
    block = 3 * line
    total = jnp.zeros((8, width), F32)
    acc_ref[0:block, :] = dot_nn(o_ref[0:block, :], wp_ref[...])
    for r in range(rows // block):
        if (r + 1) * block < rows:
            here = slice((r + 1) * block, (r + 2) * block)
            acc_ref[here, :] = dot_nn(o_ref[here, :], wp_ref[...])
        for k in range(block // line):
            at = slice(r * block + line * k, r * block + line * k + line)
            middle = x_ref[at, :].astype(F32) + acc_ref[at, :] + proj_bias
            m_ref[at, :] = middle
            unit, _ = norm_stats(middle)
            h2_ref[at, :] = (unit * gain + shift).astype(BF16)
            total = total + fold8(c_ref[at, :].astype(F32))
        if r < len(places):
            z, which, i = places[r]
            here = ds(z * piece + which * lead, lead)
            for c in range(chunks):
                w1_ref[here, width * c : width * c + width] = pieces_ref[
                    i, z, lead * (1 + c) : lead * (2 + c), :
                ]
            at = lead * (1 + chunks)
            w2_ref[ds(2 * z * tall + which * tall, tall), :] = pieces_ref[i, z, at : at + tall, :]
    put_rows(small_ref, 15, jnp.sum(total, axis=0, keepdims=True))

    count = ff // part
    buffers = ((u0_ref, da0_ref), (u1_ref, da1_ref))
    turns = [(h2_ref, h2t_ref), (c_ref, ct_ref), (o_ref, ot_ref)]
    turns = [(a, b, k) for a, b in turns for k in range(rows // LANES)]
    share = -(-len(turns) // count)

    def products(f):
        cols = slice(part * f, part * f + part)
        u_ref, da_ref = buffers[f % 2]
        u_ref[...] = dot_nn(h2_ref[...], w1_ref[:, cols])
        da_ref[...] = dot_nt(c_ref[...], w2_ref[cols, :])

    def gelu(f):
        cols = slice(part * f, part * f + part)
        u_ref, da_ref = buffers[f % 2]
        inner_bias = bias_ref[0:1, 4 * width + part * f : 4 * width + part * f + part]
        total = jnp.zeros((8, part), F32)
        c0 = 0.7978845608
        c1 = c0 * 0.044715
        for k in range(rows // line):
            at = slice(line * k, line * k + line)
            t = u_ref[at, :] + inner_bias
            square = t * t
            wave = jnp.tanh(t * (c0 + c1 * square))
            gate = 0.5 + 0.5 * wave
            a_ref[at, cols] = (t * gate).astype(BF16)
            slope = gate + t * (1.0 - wave * wave) * (0.5 * c0 + (1.5 * c1) * square)
            grad = da_ref[at, :] * slope
            du_ref[at, cols] = grad.astype(BF16)
            total = total + fold8(grad)
        put_rows(small_ref, 18 + part // LANES * f, jnp.sum(total, axis=0, keepdims=True))

    products(0)
    for f in range(count):
        if f + 1 < count:
            products(f + 1)
        gelu(f)
        for a, b, k in turns[share * f : share * f + share]:
            turn(a, b, k)

    side = width // 2
    last = []

    def put_gradient(slot, value):
        g_ref[slot] = value.astype(BF16)
        at = slice(side * slot, side * slot + side)
        last.append(start(g_ref.at[slot, ds((1 - core) * side, side)], theirs_hbm.at[at]))
        last.append(start(g_ref.at[slot, ds(core * side, side)], mine_hbm.at[at]))

    dh2_ref[...] = dot_nt(du_ref[...], w1_ref[...])
    totals = [jnp.zeros((8, width), F32)] * 3
    lines = rows // line
    per = -(-lines // (2 * chunks))
    for i in range(2 * chunks):
        inner = slice(CHUNK * (i // 2), CHUNK * (i // 2) + CHUNK)
        if i % 2 == 0:
            put_gradient(i // 2, dot_nn(h2t_ref[...], du_ref[:, inner]))
        else:
            put_gradient(chunks + i // 2, dot_nn(ct_ref[...], a_ref[:, inner]))
        for k in range(per * i, min(per * i + per, lines)):
            at = slice(line * k, line * k + line)
            unit, rstd = norm_stats(m_ref[at, :])
            grad = dh2_ref[at, :]
            inside = grad * gain
            one = jnp.mean(inside, axis=-1, keepdims=True)
            two = jnp.mean(inside * unit, axis=-1, keepdims=True)
            dm = c_ref[at, :].astype(F32) + rstd * (inside - one - unit * two)
            x_ref[at, :] = dm.astype(BF16)
            totals = [
                totals[0] + fold8(grad * unit),
                totals[1] + fold8(grad),
                totals[2] + fold8(dm),
            ]
    put_rows(small_ref, 3, jnp.sum(totals[0], axis=0, keepdims=True))
    put_rows(small_ref, 9, jnp.sum(totals[1], axis=0, keepdims=True))
    put_rows(small_ref, 12, jnp.sum(totals[2], axis=0, keepdims=True))
    last.append(start(x_ref, dy_hbm))
    put_gradient(2 * chunks, dot_nn(ot_ref[...], x_ref[...]))
    o_ref[...] = dot_nt(x_ref[...], wp_ref[...]).astype(BF16)
    last.append(start(o_ref, do_hbm))
    acc_ref[...] = dot_nn(a_ref[...], w2_ref[...])
    h2_ref[...] = (acc_ref[...] + (m_ref[...] + out_bias)).astype(BF16)
    last.append(start(h2_ref.at[0:half], outn_hbm))
    last.append(start(h2_ref.at[half:rows], outf_hbm))
    spare = side * (2 * chunks + 1)
    extra = mine_hbm.shape[0] - spare
    h2t_ref[0:extra, 0:width] = jnp.zeros((extra, width), BF16)
    for target in (mine_hbm, theirs_hbm):
        last.append(start(h2t_ref.at[0:extra, 0:width], target.at[spare : spare + extra]))
    for copy in last:
        copy.wait()


def middle(ids, tokens, swapped, mixed, cotangent, near, far, gains, shifts, ff, pieces):
    rows, width = tokens.shape
    part = 256
    act = (rows, width)
    slots = 2 * ff // CHUNK + 1
    tall = -(-(slots * (width // 2)) // (16 * pieces)) * 16 * pieces
    halves = ((tall, width), BF16)
    half = ((rows // 2, width), BF16, "hbm")
    tokens, cotangent, mixed, near = far_away(tokens, cotangent, mixed, near)
    inputs = (tokens, swapped, mixed, cotangent, near, far, gains, shifts)
    anywhere = pl.BlockSpec(memory_space=pl.ANY)
    outputs = (
        half,
        half,
        (act, BF16, "hbm"),
        (act, BF16, "hbm"),
        halves,
        halves,
        ((32, LANES), F32),
    )
    return launch(
        middle_kernel,
        ids,
        inputs,
        [anywhere] * 6 + wholes(inputs[6:]),
        outputs,
        [anywhere] * 6 + [whole((32, LANES))],
        [
            pltpu.VMEM(act, BF16),
            pltpu.VMEM(act, BF16),
            pltpu.VMEM(act, BF16),
            pltpu.VMEM((2, *near.shape), BF16),
            pltpu.VMEM((width, width), BF16),
            pltpu.VMEM((width, ff), BF16),
            pltpu.VMEM((ff, width), BF16),
            pltpu.VMEM(act, F32),
            pltpu.VMEM(act, BF16),
            pltpu.VMEM((width, rows), BF16),
            pltpu.VMEM((width, rows), BF16),
            pltpu.VMEM((width, rows), BF16),
            pltpu.VMEM(act, F32),
            pltpu.VMEM(act, F32),
            pltpu.VMEM((rows, part), F32),
            pltpu.VMEM((rows, part), F32),
            pltpu.VMEM((rows, part), F32),
            pltpu.VMEM((rows, part), F32),
            pltpu.VMEM((rows, ff), BF16),
            pltpu.VMEM((rows, ff), BF16),
            pltpu.VMEM((slots, width, CHUNK), BF16),
            pltpu.SemaphoreType.DMA((40,)),
        ],
        27,
        limit=40,
    )


def back_kernel(
    ids,
    qkv_ref,
    do_ref,
    p_ref,
    unit_ref,
    near_ref,
    far_ref,
    gain_ref,
    shift_ref,
    small_in_ref,
    ds_ref,
    dqkv_ref,
    mine_ref,
    theirs_ref,
    small_ref,
    sum_ref,
    wq_ref,
    turned_ref,
    held,
):
    width = do_ref.shape[1]
    step = pl.program_id(0)
    windows = pl.num_programs(0)
    second = step % 2
    at = ds((second * (windows // 2) + step // 2) * WTOK, WTOK)
    masks = head_masks()
    lane = lax.broadcasted_iota(I32, (8, LANES), 1) // REST
    factor = HEAD**-0.5
    for g in range(GROUPS):
        cols = slice(LANES * g, LANES * g + LANES)
        k_cols = slice(width + LANES * g, width + LANES * g + LANES)
        v_cols = slice(2 * width + LANES * g, 2 * width + LANES * g + LANES)
        q4 = qkv_ref[:, cols]
        k4 = qkv_ref[:, k_cols]
        v4 = qkv_ref[:, v_cols]
        dom = spread(do_ref[:, cols], masks)
        raw = dot_nt(v4, dom)
        parts = []
        for tile in range(5):
            sub = slice(LANES * tile, LANES * tile + LANES)
            weight = p_ref[g, :, sub].astype(F32)
            product = raw[:, sub] * weight
            dscore = product - weight * jnp.sum(product, axis=0, keepdims=True)
            parts.append(dscore.astype(BF16))
            sum_ref[second, 5 * g + tile] = dscore
        dscores = jnp.concatenate(parts, axis=1)
        dv = dot_nn(p_ref[g], dom)
        dk = dot_nn(dscores, spread(q4, masks)) * factor
        dq = fold(dot_tn(k4, dscores)) * factor
        dqkv_ref[at, cols] = dq.astype(BF16)
        dqkv_ref[at, k_cols] = dk.astype(BF16)
        dqkv_ref[at, v_cols] = dv.astype(BF16)

    @pl.when(second == 1)
    def _():
        for g in range(GROUPS):
            for tile in range(4):
                ds_ref[4 * g + tile, 0, 0:WTOK, :] = (
                    sum_ref[0, 5 * g + tile] + sum_ref[1, 5 * g + tile]
                ).astype(BF16)
            dscore = sum_ref[0, 5 * g + 4] + sum_ref[1, 5 * g + 4]
            for h in range(4):
                pieces = []
                for p in range(3):
                    total = jnp.zeros((8, LANES), F32)
                    for slot in range(8):
                        block = 8 * p + slot
                        if block < ROWBLOCKS:
                            piece = dscore[8 * block : 8 * block + 8, :]
                            turn = (16 * (slot - h)) % LANES
                            if turn:
                                piece = pltpu.roll(piece, turn, 1)
                            total = jnp.where(lane == slot, piece, total)
                    pieces.append(total)
                pieces.append(jnp.zeros((PACKED - USED, LANES), F32))
                ds_ref[4 * g + h, 0, WTOK:PACKED, :] = jnp.concatenate(pieces, axis=0).astype(BF16)

    @pl.when(step == windows - 1)
    def _():
        place_first(ids, near_ref, far_ref, wq_ref)
        rows = unit_ref.shape[0]
        for k in range(rows // LANES):
            sub = slice(LANES * k, LANES * k + LANES)
            turned_ref[:, sub] = unit_ref[sub, :].T
        gain = gain_ref[0:1, 0:width]
        shift = shift_ref[0:1, 0:width]
        gain_sum = jnp.zeros((width, 1), F32)
        shift_sum = jnp.zeros((width, 1), F32)
        for c in range(3):
            sub = slice(width * c, width * c + width)
            values = dqkv_ref[:, sub]
            product = dot_nn(turned_ref[...], values)
            total = jnp.sum(fold8(values.astype(F32)), axis=0, keepdims=True)
            weight = wq_ref[:, sub].astype(F32)
            gain_sum = gain_sum + jnp.sum(product * weight, axis=1, keepdims=True)
            shift_sum = shift_sum + jnp.sum(total * weight, axis=1, keepdims=True)
            column = jnp.broadcast_to(total, (LANES, width)).T[:, 0:1]
            held[sub, :] = (product.T * gain + column * shift).astype(BF16)
        side = mine_ref.shape[0]
        core = ids[0]
        mine_ref[...] = held[ds(core * side, side), :]
        theirs_ref[...] = held[ds((1 - core) * side, side), :]
        small_ref[...] = small_in_ref[...]
        put_rows(small_ref, 0, jnp.broadcast_to(gain_sum, (width, LANES)).T[0:1, :])
        put_rows(small_ref, 6, jnp.broadcast_to(shift_sum, (width, LANES)).T[0:1, :])


def attend_back(ids, qkv, do, p, unit, near, far, gains, shifts, small):
    rows, width = do.shape
    windows = rows // WTOK
    some = windows // 2
    place = lambda i: (i % 2) * some + i // 2
    side = ((3 * width // 2, width), BF16)
    qkv, do, p, unit = far_away(qkv, do, p, unit)
    return launch(
        back_kernel,
        ids,
        (qkv, do, p, unit, near, far, gains, shifts, small),
        [
            pl.BlockSpec((WTOK, 3 * width), lambda i, ids: (place(i), 0)),
            pl.BlockSpec((WTOK, width), lambda i, ids: (place(i), 0)),
            pl.BlockSpec((GROUPS, WTOK, SPAN), lambda i, ids: (place(i), 0, 0)),
        ]
        + wholes((unit, near, far, gains, shifts, small)),
        (
            ((HEADS, some, PACKED, LANES), BF16),
            ((rows, 3 * width), BF16),
            side,
            side,
            ((32, LANES), F32),
        ),
        (
            pl.BlockSpec((HEADS, 1, PACKED, LANES), lambda i, ids: (0, i // 2, 0, 0)),
            whole((rows, 3 * width)),
            whole(side[0]),
            whole(side[0]),
            whole((32, LANES)),
        ),
        [
            pltpu.VMEM((2, 5 * GROUPS, WTOK, LANES), F32),
            pltpu.VMEM((width, 3 * width), BF16),
            pltpu.VMEM((width, rows), BF16),
            pltpu.VMEM((3 * width, width), BF16),
        ],
        16,
        grid=(windows,),
    )


def first_back_kernel(
    ids,
    xn_ref,
    xf_ref,
    dqkv_ref,
    near_ref,
    far_ref,
    dy_ref,
    gain_ref,
    out_ref,
    own_ref,
    send_ref,
    wq_ref,
    dh1_ref,
):
    half, width = xn_ref.shape
    place_first(ids, near_ref, far_ref, wq_ref)
    dh1_ref[...] = dot_nt(dqkv_ref[...], wq_ref[...])
    gain = gain_ref[0:1, 0:width]
    send_ref[0:half, :] = out_ref[...]
    for which, (source, target) in enumerate(((xn_ref, own_ref), (xf_ref, send_ref))):

        def back_block(step, _):
            here = ds(step * WTOK, WTOK)
            at = ds(step * WTOK + which * half, WTOK)
            unit, rstd = norm_stats(source[here, :].astype(F32))
            inner = dh1_ref[at, :] * gain
            first = jnp.mean(inner, axis=-1, keepdims=True)
            second = jnp.mean(inner * unit, axis=-1, keepdims=True)
            dx = dy_ref[at, :].astype(F32) + rstd * (inner - first - unit * second)
            target[at if which else here, :] = dx.astype(BF16)
            return 0

        lax.fori_loop(0, half // WTOK, back_block, 0)


def first_back(ids, tokens, swapped, dqkv, near, far, dy, gains, out_far):
    rows, width = tokens.shape
    tokens, dy, out_far = far_away(tokens, dy, out_far)
    inputs = (tokens, swapped, dqkv, near, far, dy, gains, out_far)
    half = (rows // 2, width)
    return launch(
        first_back_kernel,
        ids,
        inputs,
        [own_half(tokens), half_of(swapped, 0)] + wholes(inputs[2:]),
        ((half, BF16, "hbm"), ((rows, width), BF16, "hbm")),
        (whole(half), whole((rows, width))),
        [pltpu.VMEM((width, 3 * width), BF16), pltpu.VMEM((rows, width), F32)],
        6,
    )


def scatter_kernel(
    ids,
    idx_ref,
    ds_ref,
    small_ref,
    qm_ref,
    qr_ref,
    *refs,
):
    outs = refs[:4]
    both, *sides, acc, table, joined = refs[4:]
    lefts, rights = sides[:2], sides[2:]
    xy = ids[1]
    rows = ds_ref.shape[0]
    highs = lefts[0].shape[0] // rows
    place = lax.broadcasted_iota(I32, (LOW, LANES), 0).astype(F32).astype(BF16)
    one = jnp.ones((LOW, LANES), BF16)
    nothing = jnp.zeros((rows, LANES), BF16)
    acc[...] = jnp.zeros_like(acc)

    def one_block(step, _):
        here = ds(step * 16, 16)
        both[...] = ds_ref[:, here, :].astype(F32).reshape(rows * 16, LANES)
        index = idx_ref[here, :]
        low = (index & (LOW - 1)).astype(F32).astype(BF16)
        high = (index // LOW).astype(F32).astype(BF16)
        product = None
        for part in range(2):
            left, right = lefts[part], rights[part]
            for j in range(8):
                k = 8 * part + j
                cols = slice(LANES * j, LANES * j + LANES)
                right[:, cols] = jnp.where(place == low[k : k + 1, :], one, jnp.zeros_like(one))
                value = both[pl.ds(k, rows, stride=16), :].astype(BF16)
                owner = jnp.broadcast_to(high[k : k + 1, :], (rows, LANES))
                for b in range(highs):
                    left[rows * b : rows * b + rows, cols] = jnp.where(
                        owner == jnp.full((rows, LANES), b, BF16), value, nothing
                    )
            found = dot_nt(left[...], right[...])
            product = found if product is None else product + found
        acc[...] += product
        return 0

    lax.fori_loop(0, idx_ref.shape[0] // 16, one_block, 0)
    table[...] = jnp.zeros_like(table)
    for tile in range(2 * highs):
        t, u = tile // 3, tile % 3
        table[rows * t : rows * t + rows, LANES * u : LANES * u + LANES] = acc[
            rows * (tile // 2) : rows * (tile // 2) + rows,
            LANES * (tile % 2) : LANES * (tile % 2) + LANES,
        ].astype(BF16)
    t, u = 2 * highs // 3, 2 * highs % 3
    table[rows * t : rows * t + 32, LANES * u : LANES * u + LANES] = small_ref[...].astype(BF16)
    joined[0 : qm_ref.shape[0], :] = (
        qm_ref[...].astype(F32) + qr_ref[...].astype(F32)
    ).astype(BF16)
    joined[qm_ref.shape[0] :, :] = table[...]
    shards, piece, _ = outs[0].shape
    for k in range(4):
        for z in range(shards):
            outs[k][z] = joined[ds(((xy ^ k) * shards + z) * piece, piece), :]


def table_gradient(ids, idx, dscores, small, q_mine, q_got, entries, shards):
    rows = dscores.shape[0]
    highs = -(-entries // LOW)
    width = q_mine.shape[1]
    pieces = 4 * shards
    table_rows = rows * (-(-(2 * highs + 1) // 3))
    piece = -(-(q_mine.shape[0] + table_rows) // (16 * pieces)) * 16
    table_rows = pieces * piece - q_mine.shape[0]
    out = ((shards, piece, width), BF16)
    return launch(
        scatter_kernel,
        ids,
        (idx, dscores, small, q_mine, q_got),
        [
            whole(idx.shape),
            whole(dscores.shape),
            whole(small.shape),
            whole(q_mine.shape),
            whole(q_got.shape),
        ],
        (out,) * 4,
        (whole(out[0]),) * 4,
        [
            pltpu.VMEM((rows * 16, LANES), F32),
            pltpu.VMEM((highs * rows, 8 * LANES), BF16),
            pltpu.VMEM((highs * rows, 8 * LANES), BF16),
            pltpu.VMEM((LOW, 8 * LANES), BF16),
            pltpu.VMEM((LOW, 8 * LANES), BF16),
            pltpu.VMEM((highs * rows, LOW), F32),
            pltpu.VMEM((table_rows, width), BF16),
            pltpu.VMEM((pieces * piece, width), BF16),
        ],
        15,
    )


def deal_kernel(count, which, ids, *refs):
    parts, outs, held = refs[:count], refs[count:-1], refs[-1]
    total = parts[0][...].astype(F32)
    for part in parts[1:]:
        total = total + part[...].astype(F32)
    held[...] = total.astype(BF16).reshape(held.shape)
    for k, out in enumerate(outs):
        out[...] = held[ids[which] ^ k]


def deal(ids, which, ways, parts):
    shape = parts[0].shape
    if len(shape) == 2:
        shape = (ways, shape[0] // ways, shape[1])
    out = (shape[1:], BF16)
    return launch(
        functools.partial(deal_kernel, len(parts), which),
        ids,
        parts,
        wholes(parts),
        (out,) * ways,
        (whole(out[0]),) * ways,
        [pltpu.VMEM(shape, BF16)],
        4,
    )


def pass_kernel(ids, a_ref, out_ref):
    out_ref[...] = a_ref[...]


def hand_on(ids, array):
    spec = whole(array.shape)
    return launch(
        pass_kernel, ids, (array,), (spec,), ((array.shape, array.dtype),), (spec,), [], 200
    )[0]


def join_kernel(*refs):
    parts, out = refs[1:-1], refs[-1]
    total = parts[0][...].astype(F32)
    for part in parts[1:]:
        total = total + part[...].astype(F32)
    out[...] = total.astype(BF16)


def join(ids, parts):
    shape = parts[0].shape
    return launch(
        join_kernel, ids, parts, wholes(parts), ((shape, BF16),), (whole(shape),), [], 4
    )[0]


def put_pieces(size, count, place, load):
    for i in range(count):
        start, end = i * size, (i + 1) * size
        while start < end:
            stop, store = place(start, end)
            if store is not None:
                store(load(i, slice(start - i * size, stop - i * size)))
            start = stop


def forward_update_kernel(
    tokens_total,
    ids,
    near_ref,
    far_ref,
    bn_ref,
    bf_ref,
    rn_ref,
    rf_ref,
    r1_ref,
    l1_ref,
    a1_ref,
    m1_ref,
    w1_ref,
    l2_ref,
    a2_ref,
    r2_ref,
    m2_ref,
    w2_ref,
    ap_ref,
    rp_ref,
    lp_ref,
    mp_ref,
    wp_ref,
    r1_out,
    l1_out,
    m1_out,
    w1_out,
    l2_out,
    r2_out,
    m2_out,
    w2_out,
    rp_out,
    lp_out,
    mp_out,
    wp_out,
    g_ref,
    y_ref,
    z_ref,
    lacc_ref,
    racc_ref,
    root_ref,
    turned_ref,
):
    c = pl.program_id(0)
    count = pl.num_programs(0)
    core, xy, s = ids[0], ids[1], ids[2]
    width = g_ref.shape[1]
    ff = count * CHUNK
    piece = l1_ref.shape[0]
    rows = ds(s * piece, piece)
    keep = shampoo_decay
    new = (1.0 - shampoo_decay) / tokens_total
    scale = 1.0 / math.sqrt(tokens_total)

    @pl.when(c == 0)
    def _():
        side = width // 2
        shards = near_ref.shape[1]
        for which, pieces in ((core, near_ref), (1 - core, far_ref)):

            def place(start, end):
                slot = start // side
                stop = min(end, (slot + 1) * side)
                if slot >= g_ref.shape[0]:
                    return end, None
                at = which * side + start - slot * side

                def store(value):
                    g_ref[slot, ds(at, value.shape[0]), :] = value

                return stop, store

            def load(i, rows):
                return pieces[xy ^ (i // shards), s ^ (i % shards), rows, :]

            put_pieces(pieces.shape[2], 4 * shards, place, load)
        half = piece // 2
        for which, ref in ((core, rn_ref), (1 - core, rf_ref)):
            for z in range(shards):
                for i in range(3):
                    root_ref[i, ds(z * piece + which * half, half), :] = ref[
                        z, half * i : half * i + half, :
                    ]
        turned_ref[0] = g_ref[s].T
        turned_ref[1] = g_ref[count + s].T
        for i in range(y_ref.shape[0]):
            y_ref[i] = dot_nn(a1_ref[...].astype(BF16), g_ref[i]).astype(BF16)
        z_ref[...] = jnp.zeros_like(z_ref)
        lacc_ref[...] = jnp.zeros_like(lacc_ref)
        racc_ref[...] = jnp.zeros_like(racc_ref)

    g1 = g_ref[c]
    g2 = g_ref[count + c]
    r1_out[...] = keep * r1_ref[...] + (new / width) * dot_nn(turned_ref[0], g1)
    l2_out[...] = keep * l2_ref[...] + (new / width) * dot_nn(turned_ref[1], g2)
    shards = bn_ref.shape[0]
    steps = count // 2

    def first_columns(which, ref):
        change = dot_nn(y_ref[0], ref[0])
        for z in range(1, shards):
            change = change + dot_nn(y_ref[z], ref[z])
        cols = pl.ds(
            pl.multiple_of(which * (ff // 2) + c % steps * CHUNK, LANES), CHUNK
        )
        momentum = shampoo_momentum * m1_ref[:, cols] + change * scale
        m1_out[:, cols] = momentum
        w1_out[:, cols] = w1_ref[:, cols] - matrix_rates[2] * momentum

    @pl.when(c < steps)
    def _():
        first_columns(core, bn_ref)

    @pl.when(c >= steps)
    def _():
        first_columns(1 - core, bf_ref)

    z_ref[...] += dot_nt(a2_ref[...].astype(BF16), g2)
    lacc_ref[...] += dot_nt(g_ref[c, rows, :], g1)
    racc_ref[...] += dot_nt(g_ref[count + c, rows, :], g2)

    @pl.when(c == count - 1)
    def _():
        l1_out[...] = keep * l1_ref[...] + (new / ff) * lacc_ref[...]
        r2_out[...] = keep * r2_ref[...] + (new / ff) * racc_ref[...]
        change = dot_nn(z_ref[...].astype(BF16), root_ref[2]) * scale
        momentum = shampoo_momentum * m2_ref[...] + change
        m2_out[...] = momentum
        w2_out[...] = w2_ref[...] - matrix_rates[3] * momentum
        gp = g_ref[2 * count]
        z_ref[...] = dot_tn(gp, gp)
        rp_out[...] = keep * rp_ref[...] + (new / width) * z_ref[rows, :]
        lp_out[...] = keep * lp_ref[...] + (new / width) * dot_nt(g_ref[2 * count, rows, :], gp)
        first = dot_nn(ap_ref[...].astype(BF16), gp).astype(BF16)
        change = dot_nn(first, root_ref[0]) * scale
        momentum = shampoo_momentum * mp_ref[...] + change
        mp_out[...] = momentum
        wp_out[...] = wp_ref[...] - matrix_rates[1] * momentum


def forward_update(
    total, ids, near, far, r_near, r_far, r1, l1, a1, m1, w1, l2, a2, r2, m2, w2, ap, rp, lp, mp, wp
):
    shards, width = near.shape[1], near.shape[3]
    count = r1.shape[1] // CHUNK
    steps = count // 2
    rank_rows = r1.shape[0]
    piece = l1.shape[0]
    assert rank_rows == CHUNK == width
    column = pl.BlockSpec((rank_rows, CHUNK), lambda c, ids: (0, c))
    updated = (r1, l1, m1, w1, l2, r2, m2, w2, rp, lp, mp, wp)
    (r_near,) = far_away(r_near)
    inputs = (
        near,
        far,
        r_near,
        r_far,
        r_near,
        r_far,
        *far_away(r1, l1, a1, m1, w1, l2, a2, r2, m2, w2, ap, rp, lp, mp, wp),
    )
    block = (shards, rank_rows, width)
    rest = (shards, rank_rows // 2, width)
    place = lambda c, ids: (0, 2 * steps, 0)
    roots = [
        pl.BlockSpec(block, lambda c, ids: (0, jnp.minimum(c, steps - 1), 0)),
        pl.BlockSpec(block, lambda c, ids: (0, jnp.maximum(c - steps, 0), 0)),
        pl.BlockSpec(rest, place),
        pl.BlockSpec(rest, place),
    ]
    return launch(
        functools.partial(forward_update_kernel, total),
        ids,
        inputs,
        wholes(inputs[:2])
        + roots
        + [column if i in (6, 11, 12) else whole(inputs[i].shape) for i in range(6, len(inputs))],
        [(a.shape, F32) for a in updated],
        [column if i in (0, 4) else whole(a.shape) for i, a in enumerate(updated)],
        [
            pltpu.VMEM((2 * count + 1, width, CHUNK), BF16),
            pltpu.VMEM((count, piece, CHUNK), BF16),
            pltpu.VMEM((rank_rows, width), F32),
            pltpu.VMEM(l1.shape, F32),
            pltpu.VMEM(r2.shape, F32),
            pltpu.VMEM((3, width, width), BF16),
            pltpu.VMEM((2, width, width), BF16),
        ],
        12,
        grid=(count,),
        limit=40,
    )


def attention_update_kernel(
    tokens_total,
    ids,
    near_ref,
    far_ref,
    rn_ref,
    rf_ref,
    aq_ref,
    rq_ref,
    lq_ref,
    mq_ref,
    wq_ref,
    rq_out,
    lq_out,
    mq_out,
    wq_out,
    square,
    g_ref,
    root_ref,
):
    core, xy, s = ids[0], ids[1], ids[2]
    piece, width = lq_ref.shape
    span = rq_ref.shape[0]
    full_width = rq_ref.shape[1]
    side = full_width // 2
    shards = near_ref.shape[1]
    for which, pieces in ((core, near_ref), (1 - core, far_ref)):

        def place(start, end):
            if start >= side:
                return end, None

            def store(value):
                g_ref[ds(which * side + start, value.shape[0]), :] = value

            return min(end, side), store

        def load(i, rows):
            return pieces[xy ^ (i // shards), s ^ (i % shards), rows, :]

        put_pieces(pieces.shape[2], 4 * shards, place, load)

    part = span // 2
    for which, ref in ((core, rn_ref), (1 - core, rf_ref)):
        for z in range(shards):
            for c in range(full_width // width):
                at = part * c
                root_ref[ds(z * span + which * part, part), width * c : width * c + width] = ref[
                    z, at : at + part, :
                ]
    rows = ds(s * piece, piece)
    some = ds(s * span, span)
    keep = shampoo_decay
    new = (1.0 - shampoo_decay) / tokens_total
    gq = g_ref[...]
    rq_out[...] = keep * rq_ref[...] + (new / width) * dot_nt(g_ref[some, :], gq)
    square[...] = dot_tn(gq, gq)
    lq_out[...] = keep * lq_ref[...] + (new / full_width) * square[rows, :]
    first = dot_nt(aq_ref[...].astype(BF16), gq).astype(BF16)
    change = dot_nn(first, root_ref[...]) * (1.0 / math.sqrt(tokens_total))
    momentum = shampoo_momentum * mq_ref[...] + change
    mq_out[...] = momentum
    wq_out[...] = wq_ref[...] - matrix_rates[0] * momentum


def attention_update(total, ids, near, far, r_near, r_far, aq, rq, lq, mq, wq):
    shards, width = near.shape[1], near.shape[3]
    (r_near,) = far_away(r_near)
    inputs = (near, far, r_near, r_far, *far_away(aq, rq, lq, mq, wq))
    q_rows = rq.size // 2 // width
    while r_near.shape[1] % q_rows or q_rows % 16:
        q_rows += 1
    last = r_near.shape[1] // q_rows - 1
    some = pl.BlockSpec((shards, q_rows, width), lambda i, ids: (0, last, 0))
    updated = (rq, lq, mq, wq)
    return launch(
        functools.partial(attention_update_kernel, total),
        ids,
        inputs,
        wholes(inputs[:2]) + [some, some] + wholes(inputs[4:]),
        [(a.shape, F32) for a in updated],
        wholes(updated),
        [
            pltpu.VMEM((width, width), F32),
            pltpu.VMEM((rq.shape[1], width), BF16),
            pltpu.VMEM((rq.shape[1], rq.shape[1]), BF16),
        ],
        3,
    )


def adam_update(parameter, first_moment, second_moment, gradient):
    new_first = adam_first * first_moment + (1.0 - adam_first) * gradient
    new_second = adam_second * second_moment + (1.0 - adam_second) * gradient * gradient
    first_hat = new_first / (1.0 - adam_first**STEP)
    second_hat = new_second / (1.0 - adam_second**STEP)
    return (
        parameter - adam_rate * first_hat / (jnp.sqrt(second_hat) + adam_eps),
        new_first,
        new_second,
    )


def table_kernel(
    tokens_total,
    skip,
    ids,
    near_ref,
    far_ref,
    t_ref,
    f_ref,
    q_ref,
    on_ref,
    in_ref,
    got_ref,
    t_out,
    f_out,
    q_out,
    v_out,
    block_ref,
    grad_ref,
    held,
    turned,
):
    core, xy, s = ids[0], ids[1], ids[2]
    heads, kinds, entries = t_ref.shape
    scale = 1.0 / math.sqrt(tokens_total)
    shards, size = near_ref.shape[1], near_ref.shape[2]
    some = kinds // 2
    width = held.shape[2]
    tiles = -(-entries // LANES)
    total = some * HEADS

    @pl.when(pl.program_id(0) == 0)
    def _():
        for i in range(skip // size, 4 * shards):
            start = i * size - skip
            for which, pieces in ((core, near_ref), (1 - core, far_ref)):
                held[which, start : start + size, :] = (
                    pieces[xy ^ (i // shards), s ^ (i % shards)].astype(F32) * scale
                )
        for h in range(HEADS):
            for u in range(turned.shape[2] // width):
                at = slice(total * u + some * h, total * u + some * h + some)
                cols = slice(width * u, width * u + width)
                turned[h, 0:some, cols] = held[0, at, :]
                turned[h, some:kinds, cols] = held[1, at, :]
        per = width // LANES
        start, at = total * (tiles // per), LANES * (tiles % per)
        v_out[...] = (
            held[0, start : start + 32, at : at + LANES]
            + held[1, start : start + 32, at : at + LANES]
        )
        half = on_ref.shape[0]
        for own, ref, at in ((on_ref, block_ref, 0), (in_ref, grad_ref, half)):
            ref[ds(core * half, half), :] = own[...]
            ref[ds((1 - core) * half, half), :] = got_ref[at : at + half, :]

    first = pl.program_id(0) * heads
    for h in range(heads):
        grad = turned[first + h, :, 0:entries]
        t_out[h], f_out[h], q_out[h] = adam_update(t_ref[h], f_ref[h], q_ref[h], grad)


def table_update(total, ids, near, far, skip, table, first, second, out_own, in_own, got):
    shards, piece, width = near.shape[1:]
    heads, kinds, entries = table.shape
    assert skip % piece == 0
    block = pl.BlockSpec((heads // 4, kinds, entries), lambda i, ids: (i, 0, 0))
    out_own, in_own = far_away(out_own, in_own)
    inputs = (near, far, *far_away(table, first, second), out_own, in_own, got)
    outputs = ((table.shape, F32),) * 3 + (((32, LANES), F32),) + ((got.shape, BF16),) * 2
    return launch(
        functools.partial(table_kernel, total, skip),
        ids,
        inputs,
        wholes(inputs[:2]) + [block] * 3 + wholes(inputs[5:]),
        outputs,
        [block] * 3 + [whole(o[0]) for o in outputs[3:]],
        [
            pltpu.VMEM((2, 4 * shards * piece - skip, width), F32),
            pltpu.VMEM((heads, kinds, -(-entries // width) * width), F32),
        ],
        3,
        grid=(4,),
    )


XY = ("y", "x")


def swap(array, axes, k, size):
    return lax.ppermute(array, axes, [(i, i ^ k) for i in range(size)])


def after(array, *others):
    return lax.optimization_barrier((array, *others))[0]


def per_device(
    tokens,
    cotangent,
    rel_index,
    qkv_weight,
    proj_weight,
    fc1_weight,
    fc2_weight,
    qkv_momentum,
    proj_momentum,
    fc1_momentum,
    fc2_momentum,
    qkv_left,
    qkv_right,
    proj_left,
    proj_right,
    fc1_left,
    fc1_right,
    fc2_left,
    fc2_right,
    qkv_left_root,
    qkv_right_root,
    proj_left_root,
    proj_right_root,
    fc1_left_root,
    fc1_right_root,
    fc2_left_root,
    fc2_right_root,
    norm_gains,
    biases,
    bias_table,
    gains_first,
    gains_second,
    biases_first,
    biases_second,
    table_first,
    table_second,
):
    shards = lax.axis_size("fsdp")
    outer = lax.axis_size("outer")
    core = lax.axis_index("core")
    z = lax.axis_index("fsdp")
    xy = lax.axis_index("y") * 2 + lax.axis_index("x")
    ids = jnp.stack([core, xy, z]).astype(I32)
    rows, width = tokens.shape
    total = rows * outer * 8 * shards
    kinds, heads, entries = bias_table.shape
    assert rows // WTOK == kinds and heads == HEADS and shards == 4
    ff = fc1_weight.shape[1]

    pieces = 4 * shards

    def scatter_xy(parts, *before):
        parts = [parts[0]] + [swap(parts[k], XY, k, 4) for k in range(1, 4)]
        return deal(after(ids, *before), 2, shards, parts)

    def scatter_z(parts, *before):
        parts = [parts[0]] + [swap(parts[k], "fsdp", k, shards) for k in range(1, shards)]
        piece = join(after(ids, *before), parts)
        return lax.psum(piece, "outer") if outer > 1 else piece

    def gather_z(piece):
        return jnp.stack([piece] + [swap(piece, "fsdp", k, shards) for k in range(1, shards)])

    def gather_xy(piece, *before):
        pieces = [piece] + [swap(piece, XY, k, 4) for k in range(1, 4)]
        return jnp.stack([after(pieces[0], *before)] + pieces[1:])

    table_of = lambda array: array.transpose(1, 0, 2)
    table, table_f, table_q = map(table_of, (bias_table, table_first, table_second))

    first, others_own, swapped = pack(
        ids, tokens, cotangent, qkv_weight, proj_weight, fc1_weight, fc2_weight
    )
    swapped = swap(swapped, "core", 1, 2)
    roots_own = pack_roots(
        after(ids, first),
        proj_right_root,
        fc1_left_root,
        fc2_right_root,
        qkv_right_root,
        fc1_right_root,
    )
    others = lax.all_gather(others_own, "fsdp", axis=0)

    gains = norm_gains.reshape(1, -1)
    shifts = biases.reshape(1, -1)
    bias, idx = bias_gather(after(ids, first, roots_own), rel_index, table)
    first_near = [swap(first, "fsdp", k, shards) for k in range(1, shards)]
    first_near = jnp.stack([after(first, bias)] + first_near)
    first_far = swap(first_near, "core", 1, 2)
    qkv, unit, p, mixed = attend(
        ids, tokens, swapped, first_near, first_far, gains, shifts, bias
    )
    others_far = swap(after(others, mixed), "core", 1, 2)
    roots = lax.all_gather(after(roots_own, mixed), "fsdp", axis=0)
    out_own, out_far, dy, do, g_mine, g_theirs, small = middle(
        ids, tokens, swapped, mixed, cotangent, others, others_far, gains, shifts, ff, pieces
    )
    g_got = swap(g_theirs, "core", 1, 2)
    small = hand_on(ids, small)
    g_parts = deal(after(ids, small), 1, 4, (g_mine, g_got))
    g_parts = [part.reshape(shards, -1, width) for part in g_parts]
    dscores, dqkv, q_mine, q_theirs, small = attend_back(
        after(ids, *g_parts), qkv, do, p, unit, first_near, first_far, gains, shifts, small
    )
    q_got = swap(q_theirs, "core", 1, 2)
    g_parts = scatter_xy(g_parts, q_mine)
    parts = table_gradient(
        after(ids, *g_parts),
        idx,
        dscores.reshape(-1, PACKED, LANES),
        small,
        q_mine,
        q_got,
        entries,
        shards,
    )
    g_piece = scatter_z(g_parts, parts[0])
    in_own, in_far = first_back(
        after(ids, g_piece), tokens, swapped, dqkv, first_near, first_far, dy, gains, out_far
    )
    parts = scatter_xy(parts, in_far)
    got = swap(in_far, "core", 1, 2)
    g_piece = gather_z(g_piece)
    piece = scatter_z(parts, g_piece)
    g_near = gather_xy(g_piece, piece)
    piece = gather_z(piece)
    near = gather_xy(piece, g_near)
    far = swap(near, "core", 1, 2)
    roots_far = swap(after(roots, far, got), "core", 1, 2)
    g_far = swap(after(g_near, far, got), "core", 1, 2)
    *table_out, vectors, block_output, input_grad = table_update(
        total,
        after(ids, near),
        near,
        far,
        3 * width // 2,
        table,
        table_f,
        table_q,
        out_own,
        in_own,
        got,
    )
    rq, lq, mq, wq = attention_update(
        total,
        ids,
        near,
        far,
        roots,
        roots_far,
        qkv_left_root,
        qkv_right,
        qkv_left,
        qkv_momentum,
        qkv_weight,
    )
    r1, l1, m1, w1, l2, r2, m2, w2, rp, lp, mp, wp = forward_update(
        total,
        after(ids, rq),
        g_near,
        g_far,
        roots,
        roots_far,
        fc1_right,
        fc1_left,
        fc1_left_root,
        fc1_momentum,
        fc1_weight,
        fc2_left,
        fc2_left_root,
        fc2_right,
        fc2_momentum,
        fc2_weight,
        proj_left_root,
        proj_right,
        proj_left,
        proj_momentum,
        proj_weight,
    )
    table_out = [table_of(array) for array in table_out]
    vectors = vectors.reshape(-1)
    size = norm_gains.shape[0]
    gains_out = adam_update(norm_gains, gains_first, gains_second, vectors[:size])
    biases_out = adam_update(
        biases, biases_first, biases_second, vectors[size : size + biases.shape[0]]
    )
    return (
        block_output,
        input_grad,
        wq,
        wp,
        w1,
        w2,
        mq,
        mp,
        m1,
        m2,
        lq,
        rq,
        lp,
        rp,
        l1,
        r1,
        l2,
        r2,
        gains_out[0],
        biases_out[0],
        table_out[0],
        gains_out[1],
        biases_out[1],
        table_out[1],
        gains_out[2],
        biases_out[2],
        table_out[2],
    )


def solution(mesh):
    dp, fsdp = mesh.devices.shape
    split_mesh = jax.sharding.Mesh(
        mesh.devices.reshape(dp // 8, 2, 2, 2, fsdp), ("outer", "y", "x", "core", "fsdp")
    )
    rows = P(("outer", "y", "x", "core", "fsdp"), None)
    shard = P("fsdp", None)
    return jax.shard_map(
        per_device,
        mesh=split_mesh,
        in_specs=(rows, rows) + (P(),) + (shard,) * 24 + (P(),) * 9,
        out_specs=(rows, rows) + (shard,) * 16 + (P(),) * 9,
        check_vma=False,
    )
```

```python
import functools
import math

import jax
import jax.numpy as jnp
from jax import lax
from jax.experimental import pallas as pl
from jax.experimental.pallas import tpu as pltpu
from jax.sharding import PartitionSpec as P

HEADS = 12
HEAD = 32
STEP = 5
WTOK = 144
LANES = 128
GROUPS = HEADS // 4
SPAN = 5 * LANES
REST = WTOK - LANES
ROWBLOCKS = WTOK // 8
CHUNK = 384
LOG2E = 1.4426950408889634

norm_eps = 1e-05
adam_first = 0.9
adam_second = 0.999
adam_eps = 1e-08
adam_rate = 0.3
shampoo_decay = 0.5
shampoo_momentum = 0.9
matrix_rates = (0.02, 0.1, 0.02, 0.02)

F32 = jnp.float32
BF16 = jnp.bfloat16
I32 = jnp.int32


def dot_nn(a, b):
    return lax.dot_general(a, b, (((1,), (0,)), ((), ())), preferred_element_type=F32)


def dot_nt(a, b):
    return lax.dot_general(a, b, (((1,), (1,)), ((), ())), preferred_element_type=F32)


def dot_tn(a, b):
    return lax.dot_general(a, b, (((0,), (0,)), ((), ())), preferred_element_type=F32)


PACKED = 176
USED = 168
LOW = 256


def launch(body, ids, inputs, in_specs, outputs, out_specs, scratch, micros, grid=(1,), limit=32):
    micros = max(micros, 20) if micros > 3 else 3
    return pl.pallas_call(
        body,
        out_shape=tuple(
            pltpu.HBM(out[0], out[1]) if len(out) > 2 else jax.ShapeDtypeStruct(*out)
            for out in outputs
        ),
        grid_spec=pltpu.PrefetchScalarGridSpec(
            num_scalar_prefetch=1,
            grid=grid,
            in_specs=in_specs,
            out_specs=tuple(out_specs),
            scratch_shapes=scratch,
        ),
        compiler_params=pltpu.CompilerParams(vmem_limit_bytes=limit * 2**20),
        cost_estimate=pl.CostEstimate(
            flops=int(micros * 5e8), bytes_accessed=int(micros * 3e6), transcendentals=0
        ),
    )(ids, *inputs)


def far_away(*arrays):
    return [pltpu.with_memory_space_constraint(array, pltpu.HBM) for array in arrays]


def whole(shape):
    return pl.BlockSpec(tuple(shape), lambda *_: (0,) * len(shape))


def wholes(arrays):
    return [whole(array.shape) for array in arrays]


def ds(start, size, multiple=16):
    return pl.ds(pl.multiple_of(start, multiple), size)


def pack_kernel(ids, x, c, wq, wp, w1, w2, first, others, swapped):
    core = ids[0]
    half = first.shape[0]
    width = others.shape[1]
    here = ds(core * half, half)
    first[...] = wq[here, :].astype(BF16)
    others[0:half, :] = wp[here, :].astype(BF16)
    chunks = w1.shape[1] // width
    for i in range(chunks):
        others[half * (1 + i) : half * (2 + i), :] = w1[
            here, width * i : width * i + width
        ].astype(BF16)
    tall = w2.shape[0] // 2
    start = half * (1 + chunks)
    others[start : start + tall, :] = w2[ds(core * tall, tall), :].astype(BF16)
    rows = x.shape[0] // 2
    there = ds((1 - core) * rows, rows)
    swapped[0:rows, :] = x[there, :]
    swapped[rows : 2 * rows, :] = c[there, :]


def pack(ids, tokens, cotangent, wq, wp, w1, w2):
    piece, width = wp.shape
    half = piece // 2
    rows = half * (1 + w1.shape[1] // width) + w2.shape[0] // 2
    inputs = far_away(tokens, cotangent, wq, wp, w1, w2)
    outputs = (((half, wq.shape[1]), BF16), ((rows, width), BF16), (tokens.shape, BF16))
    return launch(
        pack_kernel, ids, inputs, wholes(inputs), outputs, [whole(o[0]) for o in outputs], [], 4
    )


def pack_roots_kernel(ids, bp, a1, b2, bq, b1, roots):
    core = ids[0]
    piece, width = bp.shape
    half = piece // 2
    here = ds(core * half, half)
    tall, side = b1.shape[0], b1.shape[1] // 2
    at = 0
    for i in range(side // width):
        cols = pl.ds(pl.multiple_of(core * side + width * i, LANES), width)
        roots[at : at + tall, :] = b1[:, cols].astype(BF16)
        at += tall
    for i, root in enumerate((bp, a1, b2)):
        roots[at + half * i : at + half * i + half, :] = root[here, :].astype(BF16)
    at += 3 * half
    span = bq.shape[0] // 2
    for i in range(bq.shape[1] // width):
        roots[at : at + span, :] = bq[
            ds(core * span, span), width * i : width * i + width
        ].astype(BF16)
        at += span


def pack_roots(ids, bp, a1, b2, bq, b1):
    piece, width = bp.shape
    inputs = far_away(bp, a1, b2, bq, b1)
    rows = (b1.size + bq.size) // 2 // width + 3 * piece // 2
    assert rows % 32 == 0 and bq.size // width <= rows
    out = ((rows, width), BF16, "hbm")
    return launch(
        pack_roots_kernel, ids, inputs, wholes(inputs), (out,), (whole(out[0]),), [], 4
    )[0]


def bias_kernel(ids, rel_ref, table_ref, out_ref, idx_ref, square, wide, left, right, held):
    step = pl.program_id(0)
    heads, kinds, entries = table_ref.shape
    some = kinds // 2
    rows = some * heads
    highs = left.shape[0] // rows

    @pl.when(step == 0)
    def _():
        square[...] = jnp.zeros_like(square)
        square[0:WTOK, 0:WTOK] = rel_ref[...]
        turned = square[...].T
        idx_ref[0:WTOK, :] = turned[0:WTOK, 0:LANES]
        tail = turned[0:WTOK, LANES : 2 * LANES]
        for p in range(3):
            total = jnp.zeros((8, LANES), I32)
            for g in range(8):
                block = 8 * p + g
                if block < ROWBLOCKS:
                    piece = tail[8 * block : 8 * block + 8, :]
                    total = total + (pltpu.roll(piece, 16 * g, 1) if g else piece)
            idx_ref[WTOK + 8 * p : WTOK + 8 * p + 8, :] = total
        idx_ref[USED:PACKED, :] = jnp.zeros((PACKED - USED, LANES), I32)
        wide[...] = jnp.zeros_like(wide)
        for h in range(heads):
            mine = jnp.where(ids[0] == 0, table_ref[h, 0:some, :], table_ref[h, some:kinds, :])
            wide[some * h : some * h + some, 0:entries] = mine * LOG2E
        for b in range(highs):
            left[rows * b : rows * b + rows, :] = wide[:, LOW * b : LOW * b + LOW].astype(BF16)

    index = idx_ref[ds(step * 16, 16), :]
    low = (index & (LOW - 1)).astype(F32).astype(BF16)
    high = index // LOW
    place = lax.broadcasted_iota(I32, (LOW, LANES), 0).astype(F32).astype(BF16)
    one = jnp.ones((LOW, LANES), BF16)
    for k in range(16):
        right[:, LANES * k : LANES * k + LANES] = jnp.where(
            place == low[k : k + 1, :], one, jnp.zeros_like(one)
        )
    for k in range(0, 16, 2):
        found = dot_nn(left[...], right[:, LANES * k : LANES * k + 2 * LANES])
        for j in range(2):
            cols = slice(LANES * j, LANES * j + LANES)
            owner = high[k + j : k + j + 1, :]
            value = found[0:rows, cols]
            for b in range(1, highs):
                value = jnp.where(owner == b, found[rows * b : rows * b + rows, cols], value)
            held[pl.ds(k + j, rows, stride=16), :] = value
    out_ref[...] = held[...].reshape(rows, 16, LANES).astype(BF16)


def bias_gather(ids, rel_index, bias_table):
    heads, kinds, entries = bias_table.shape
    rows = kinds // 2 * heads
    highs = -(-entries // LOW)
    return launch(
        bias_kernel,
        ids,
        far_away(rel_index, bias_table),
        [
            whole(rel_index.shape),
            whole(bias_table.shape),
        ],
        (((rows, PACKED, LANES), BF16), ((PACKED, LANES), I32)),
        (pl.BlockSpec((rows, 16, LANES), lambda i, ids: (0, i, 0)), whole((PACKED, LANES))),
        [
            pltpu.VMEM((256, 256), I32),
            pltpu.VMEM((rows, highs * LOW), F32),
            pltpu.VMEM((highs * rows, LOW), BF16),
            pltpu.VMEM((LOW, 16 * LANES), BF16),
            pltpu.VMEM((rows * 16, LANES), F32),
        ],
        14,
        grid=(PACKED // 16,),
    )


def head_masks():
    lane = lax.broadcasted_iota(I32, (1, LANES), 1)
    return [(lane // HEAD == h).astype(F32).astype(BF16) for h in range(4)]


def spread(tile, masks):
    pieces = [tile[0:LANES] * masks[h] for h in range(4)]
    pieces += [tile[LANES:WTOK] * masks[h] for h in range(4)]
    pieces.append(jnp.zeros((64, LANES), BF16))
    return jnp.concatenate(pieces, axis=0)


def fold(turned):
    main = jnp.concatenate(
        [turned[HEAD * h : HEAD * h + HEAD, LANES * h : LANES * h + LANES] for h in range(4)],
        axis=0,
    ).T
    tail = turned[:, 4 * LANES : 5 * LANES]
    row = lax.broadcasted_iota(I32, tail.shape, 0) // HEAD
    place = lax.broadcasted_iota(I32, tail.shape, 1) // REST
    tail = jnp.where(row == place, tail, 0.0).T
    rest = tail[0:16] + tail[16:32] + tail[32:48] + tail[48:64]
    return jnp.concatenate([main, rest], axis=0)


def norm_stats(values):
    mean = jnp.mean(values, axis=-1, keepdims=True)
    centre = values - mean
    spread_of = jnp.mean(centre * centre, axis=-1, keepdims=True)
    rstd = lax.rsqrt(spread_of + norm_eps)
    return centre * rstd, rstd


def place_first(ids, near_ref, far_ref, full_ref):
    core, z = ids[0], ids[2]
    shards, half, _ = near_ref.shape
    for k in range(shards):
        base = (z ^ k) * (2 * half)
        full_ref[ds(base + core * half, half), :] = near_ref[k]
        full_ref[ds(base + (1 - core) * half, half), :] = far_ref[k]


def attend_kernel(
    ids,
    xn_ref,
    xf_ref,
    near_ref,
    far_ref,
    gain_ref,
    shift_ref,
    table_ref,
    qkv_ref,
    unit_ref,
    p_ref,
    o_ref,
    wq_ref,
    h1_ref,
):
    half, width = xn_ref.shape
    window = pl.program_id(0)

    @pl.when(window == 0)
    def _():
        place_first(ids, near_ref, far_ref, wq_ref)
        gain = gain_ref[0:1, 0:width]
        shift = shift_ref[0:1, 0:width]
        for which, ref in enumerate((xn_ref, xf_ref)):

            def norm_block(step, _):
                at = ds(step * WTOK + which * half, WTOK)
                unit, _ = norm_stats(ref[ds(step * WTOK, WTOK), :].astype(F32))
                unit_ref[at, :] = unit.astype(BF16)
                h1_ref[at, :] = (unit * gain + shift).astype(BF16)
                return 0

            lax.fori_loop(0, half // WTOK, norm_block, 0)
        for c in range(3):
            cols = slice(c * width, (c + 1) * width)
            qkv_ref[:, cols] = dot_nn(h1_ref[...], wq_ref[:, cols]).astype(BF16)

    at = ds(window * WTOK, WTOK)
    masks = head_masks()
    lane = lax.broadcasted_iota(I32, (8, LANES), 1) // REST
    for g in range(GROUPS):
        q4 = qkv_ref[at, LANES * g : LANES * g + LANES]
        k4 = qkv_ref[at, width + LANES * g : width + LANES * g + LANES]
        v4 = qkv_ref[at, 2 * width + LANES * g : 2 * width + LANES * g + LANES]
        raw = dot_nt(k4, spread(q4, masks))
        tails = [table_ref[4 * g + h, 0, WTOK:PACKED, :].astype(F32) for h in range(4)]
        pieces = []
        for block in range(ROWBLOCKS):
            p, slot = block // 8, block % 8
            total = jnp.zeros((8, LANES), F32)
            for h in range(4):
                piece = tails[h][8 * p : 8 * p + 8, :]
                turn = (16 * (h - slot)) % LANES
                if turn:
                    piece = pltpu.roll(piece, turn, 1)
                total = jnp.where(lane == h, piece, total)
            pieces.append(total)
        tail = jnp.concatenate(pieces, axis=0)
        for tile in range(5):
            cols = slice(LANES * tile, LANES * tile + LANES)
            offset = table_ref[4 * g + tile, 0, 0:WTOK, :].astype(F32) if tile < 4 else tail
            score = raw[:, cols] * (HEAD**-0.5 * LOG2E) + offset
            top = jnp.max(score, axis=0, keepdims=True)
            weight = jnp.exp2(score - top)
            total = jnp.sum(weight, axis=0, keepdims=True)
            p_ref[g, :, cols] = (weight * (1.0 / total)).astype(BF16)
        o_ref[:, LANES * g : LANES * g + LANES] = fold(dot_tn(v4, p_ref[g])).astype(BF16)


def own_half(array):
    return pl.BlockSpec((array.shape[0] // 2, array.shape[1]), lambda i, ids: (ids[0], 0))


def half_of(array, which):
    return pl.BlockSpec((array.shape[0] // 2, array.shape[1]), lambda i, ids: (which, 0))


def attend(ids, tokens, swapped, near, far, gains, shifts, table):
    rows, width = tokens.shape
    windows = rows // WTOK
    some = windows // 2
    (tokens,) = far_away(tokens)
    return launch(
        attend_kernel,
        ids,
        (
            tokens,
            swapped,
            near,
            far,
            gains,
            shifts,
            table.reshape(HEADS, some, PACKED, LANES),
        ),
        [
            own_half(tokens),
            half_of(swapped, 0),
            whole(near.shape),
            whole(far.shape),
            whole(gains.shape),
            whole(shifts.shape),
            pl.BlockSpec((HEADS, 1, PACKED, LANES), lambda i, ids: (0, i % some, 0, 0)),
        ],
        (
            ((rows, 3 * width), BF16, "hbm"),
            ((rows, width), BF16, "hbm"),
            ((windows * GROUPS, WTOK, SPAN), BF16, "hbm"),
            ((rows, width), BF16, "hbm"),
        ),
        (
            whole((rows, 3 * width)),
            whole((rows, width)),
            pl.BlockSpec((GROUPS, WTOK, SPAN), lambda i, ids: (i, 0, 0)),
            pl.BlockSpec((WTOK, width), lambda i, ids: (i, 0)),
        ),
        [pltpu.VMEM((width, 3 * width), BF16), pltpu.VMEM((rows, width), BF16)],
        3,
        grid=(windows,),
    )


def fold8(values):
    return jnp.sum(values.reshape(values.shape[0] // 8, 8, values.shape[1]), axis=0)


def put_rows(ref, start, row):
    for k in range(row.shape[1] // LANES):
        ref[start + k : start + k + 1, :] = row[:, LANES * k : LANES * k + LANES]


def middle_kernel(
    ids,
    x_hbm,
    swap_ref,
    o_hbm,
    c_hbm,
    near_hbm,
    far_hbm,
    gain_ref,
    bias_ref,
    outn_hbm,
    outf_hbm,
    dy_hbm,
    do_hbm,
    mine_hbm,
    theirs_hbm,
    small_ref,
    x_ref,
    o_ref,
    c_ref,
    pieces_ref,
    wp_ref,
    w1_ref,
    w2_ref,
    m_ref,
    h2_ref,
    h2t_ref,
    ct_ref,
    ot_ref,
    acc_ref,
    dh2_ref,
    u0_ref,
    u1_ref,
    da0_ref,
    da1_ref,
    a_ref,
    du_ref,
    g_ref,
    sem,
):
    core = ids[0]
    rows, width = o_ref.shape
    half = rows // 2
    ff = w1_ref.shape[1]
    part = u0_ref.shape[1]
    shards = near_hbm.shape[0]
    piece = width // shards
    used = []

    def start(source, target):
        copy = pltpu.make_async_copy(source, target, sem.at[len(used)])
        used.append(copy)
        copy.start()
        return copy

    own = ds(core * half, half)
    lead, tall = piece // 2, ff // shards // 2
    chunks = ff // width
    first = [
        start(near_hbm, pieces_ref.at[0]),
        start(far_hbm, pieces_ref.at[1]),
        start(o_hbm, o_ref),
        start(x_hbm.at[own], x_ref.at[0:half]),
        start(swap_ref.at[0:half], x_ref.at[half:rows]),
    ]
    second = [
        start(c_hbm.at[own], c_ref.at[0:half]),
        start(swap_ref.at[half:rows], c_ref.at[half:rows]),
    ]
    gain = gain_ref[0:1, width : 2 * width]
    shift = bias_ref[0:1, width : 2 * width]
    proj_bias = bias_ref[0:1, 2 * width : 3 * width]
    out_bias = bias_ref[0:1, 3 * width : 4 * width]
    small_ref[...] = jnp.zeros_like(small_ref)
    for copy in first:
        copy.wait()
    places = [
        (z, which, i) for z in range(shards) for i, which in enumerate((core, 1 - core))
    ]
    for z, which, i in places:
        wp_ref[ds(z * piece + which * lead, lead), :] = pieces_ref[i, z, 0:lead, :]
    for copy in second:
        copy.wait()

    def turn(source, target, k):
        cols = slice(LANES * k, LANES * k + LANES)
        target[:, cols] = source[cols, :].T

    line = 48
    block = 3 * line
    total = jnp.zeros((8, width), F32)
    acc_ref[0:block, :] = dot_nn(o_ref[0:block, :], wp_ref[...])
    for r in range(rows // block):
        if (r + 1) * block < rows:
            here = slice((r + 1) * block, (r + 2) * block)
            acc_ref[here, :] = dot_nn(o_ref[here, :], wp_ref[...])
        for k in range(block // line):
            at = slice(r * block + line * k, r * block + line * k + line)
            middle = x_ref[at, :].astype(F32) + acc_ref[at, :] + proj_bias
            m_ref[at, :] = middle
            unit, _ = norm_stats(middle)
            h2_ref[at, :] = (unit * gain + shift).astype(BF16)
            total = total + fold8(c_ref[at, :].astype(F32))
        if r < len(places):
            z, which, i = places[r]
            here = ds(z * piece + which * lead, lead)
            for c in range(chunks):
                w1_ref[here, width * c : width * c + width] = pieces_ref[
                    i, z, lead * (1 + c) : lead * (2 + c), :
                ]
            at = lead * (1 + chunks)
            w2_ref[ds(2 * z * tall + which * tall, tall), :] = pieces_ref[i, z, at : at + tall, :]
    put_rows(small_ref, 15, jnp.sum(total, axis=0, keepdims=True))

    count = ff // part
    buffers = ((u0_ref, da0_ref), (u1_ref, da1_ref))
    turns = [(h2_ref, h2t_ref), (c_ref, ct_ref), (o_ref, ot_ref)]
    turns = [(a, b, k) for a, b in turns for k in range(rows // LANES)]
    share = -(-len(turns) // count)

    def products(f):
        cols = slice(part * f, part * f + part)
        u_ref, da_ref = buffers[f % 2]
        u_ref[...] = dot_nn(h2_ref[...], w1_ref[:, cols])
        da_ref[...] = dot_nt(c_ref[...], w2_ref[cols, :])

    def gelu(f):
        cols = slice(part * f, part * f + part)
        u_ref, da_ref = buffers[f % 2]
        inner_bias = bias_ref[0:1, 4 * width + part * f : 4 * width + part * f + part]
        total = jnp.zeros((8, part), F32)
        c0 = 0.7978845608
        c1 = c0 * 0.044715
        for k in range(rows // line):
            at = slice(line * k, line * k + line)
            t = u_ref[at, :] + inner_bias
            square = t * t
            wave = jnp.tanh(t * (c0 + c1 * square))
            gate = 0.5 + 0.5 * wave
            a_ref[at, cols] = (t * gate).astype(BF16)
            slope = gate + t * (1.0 - wave * wave) * (0.5 * c0 + (1.5 * c1) * square)
            grad = da_ref[at, :] * slope
            du_ref[at, cols] = grad.astype(BF16)
            total = total + fold8(grad)
        put_rows(small_ref, 18 + part // LANES * f, jnp.sum(total, axis=0, keepdims=True))

    products(0)
    for f in range(count):
        if f + 1 < count:
            products(f + 1)
        gelu(f)
        for a, b, k in turns[share * f : share * f + share]:
            turn(a, b, k)

    side = width // 2
    last = []

    def put_gradient(slot, value):
        g_ref[slot] = value.astype(BF16)
        at = slice(side * slot, side * slot + side)
        last.append(start(g_ref.at[slot, ds((1 - core) * side, side)], theirs_hbm.at[at]))
        last.append(start(g_ref.at[slot, ds(core * side, side)], mine_hbm.at[at]))

    dh2_ref[...] = dot_nt(du_ref[...], w1_ref[...])
    totals = [jnp.zeros((8, width), F32)] * 3
    lines = rows // line
    per = -(-lines // (2 * chunks))
    for i in range(2 * chunks):
        inner = slice(CHUNK * (i // 2), CHUNK * (i // 2) + CHUNK)
        if i % 2 == 0:
            put_gradient(i // 2, dot_nn(h2t_ref[...], du_ref[:, inner]))
        else:
            put_gradient(chunks + i // 2, dot_nn(ct_ref[...], a_ref[:, inner]))
        for k in range(per * i, min(per * i + per, lines)):
            at = slice(line * k, line * k + line)
            unit, rstd = norm_stats(m_ref[at, :])
            grad = dh2_ref[at, :]
            inside = grad * gain
            one = jnp.mean(inside, axis=-1, keepdims=True)
            two = jnp.mean(inside * unit, axis=-1, keepdims=True)
            dm = c_ref[at, :].astype(F32) + rstd * (inside - one - unit * two)
            x_ref[at, :] = dm.astype(BF16)
            totals = [
                totals[0] + fold8(grad * unit),
                totals[1] + fold8(grad),
                totals[2] + fold8(dm),
            ]
    put_rows(small_ref, 3, jnp.sum(totals[0], axis=0, keepdims=True))
    put_rows(small_ref, 9, jnp.sum(totals[1], axis=0, keepdims=True))
    put_rows(small_ref, 12, jnp.sum(totals[2], axis=0, keepdims=True))
    last.append(start(x_ref, dy_hbm))
    put_gradient(2 * chunks, dot_nn(ot_ref[...], x_ref[...]))
    o_ref[...] = dot_nt(x_ref[...], wp_ref[...]).astype(BF16)
    last.append(start(o_ref, do_hbm))
    acc_ref[...] = dot_nn(a_ref[...], w2_ref[...])
    h2_ref[...] = (acc_ref[...] + (m_ref[...] + out_bias)).astype(BF16)
    last.append(start(h2_ref.at[0:half], outn_hbm))
    last.append(start(h2_ref.at[half:rows], outf_hbm))
    spare = side * (2 * chunks + 1)
    extra = mine_hbm.shape[0] - spare
    h2t_ref[0:extra, 0:width] = jnp.zeros((extra, width), BF16)
    for target in (mine_hbm, theirs_hbm):
        last.append(start(h2t_ref.at[0:extra, 0:width], target.at[spare : spare + extra]))
    for copy in last:
        copy.wait()


def middle(ids, tokens, swapped, mixed, cotangent, near, far, gains, shifts, ff, pieces):
    rows, width = tokens.shape
    part = 256
    act = (rows, width)
    slots = 2 * ff // CHUNK + 1
    tall = -(-(slots * (width // 2)) // (16 * pieces)) * 16 * pieces
    halves = ((tall, width), BF16)
    half = ((rows // 2, width), BF16, "hbm")
    tokens, cotangent, mixed, near = far_away(tokens, cotangent, mixed, near)
    inputs = (tokens, swapped, mixed, cotangent, near, far, gains, shifts)
    anywhere = pl.BlockSpec(memory_space=pl.ANY)
    outputs = (
        half,
        half,
        (act, BF16, "hbm"),
        (act, BF16, "hbm"),
        halves,
        halves,
        ((32, LANES), F32),
    )
    return launch(
        middle_kernel,
        ids,
        inputs,
        [anywhere] * 6 + wholes(inputs[6:]),
        outputs,
        [anywhere] * 6 + [whole((32, LANES))],
        [
            pltpu.VMEM(act, BF16),
            pltpu.VMEM(act, BF16),
            pltpu.VMEM(act, BF16),
            pltpu.VMEM((2, *near.shape), BF16),
            pltpu.VMEM((width, width), BF16),
            pltpu.VMEM((width, ff), BF16),
            pltpu.VMEM((ff, width), BF16),
            pltpu.VMEM(act, F32),
            pltpu.VMEM(act, BF16),
            pltpu.VMEM((width, rows), BF16),
            pltpu.VMEM((width, rows), BF16),
            pltpu.VMEM((width, rows), BF16),
            pltpu.VMEM(act, F32),
            pltpu.VMEM(act, F32),
            pltpu.VMEM((rows, part), F32),
            pltpu.VMEM((rows, part), F32),
            pltpu.VMEM((rows, part), F32),
            pltpu.VMEM((rows, part), F32),
            pltpu.VMEM((rows, ff), BF16),
            pltpu.VMEM((rows, ff), BF16),
            pltpu.VMEM((slots, width, CHUNK), BF16),
            pltpu.SemaphoreType.DMA((40,)),
        ],
        27,
        limit=40,
    )


def back_kernel(
    ids,
    qkv_ref,
    do_ref,
    p_ref,
    unit_ref,
    near_ref,
    far_ref,
    gain_ref,
    shift_ref,
    small_in_ref,
    ds_ref,
    dqkv_ref,
    mine_ref,
    theirs_ref,
    small_ref,
    sum_ref,
    wq_ref,
    turned_ref,
    held,
):
    width = do_ref.shape[1]
    step = pl.program_id(0)
    windows = pl.num_programs(0)
    second = step % 2
    at = ds((second * (windows // 2) + step // 2) * WTOK, WTOK)
    masks = head_masks()
    lane = lax.broadcasted_iota(I32, (8, LANES), 1) // REST
    factor = HEAD**-0.5
    for g in range(GROUPS):
        cols = slice(LANES * g, LANES * g + LANES)
        k_cols = slice(width + LANES * g, width + LANES * g + LANES)
        v_cols = slice(2 * width + LANES * g, 2 * width + LANES * g + LANES)
        q4 = qkv_ref[:, cols]
        k4 = qkv_ref[:, k_cols]
        v4 = qkv_ref[:, v_cols]
        dom = spread(do_ref[:, cols], masks)
        raw = dot_nt(v4, dom)
        parts = []
        for tile in range(5):
            sub = slice(LANES * tile, LANES * tile + LANES)
            weight = p_ref[g, :, sub].astype(F32)
            product = raw[:, sub] * weight
            dscore = product - weight * jnp.sum(product, axis=0, keepdims=True)
            parts.append(dscore.astype(BF16))
            sum_ref[second, 5 * g + tile] = dscore
        dscores = jnp.concatenate(parts, axis=1)
        dv = dot_nn(p_ref[g], dom)
        dk = dot_nn(dscores, spread(q4, masks)) * factor
        dq = fold(dot_tn(k4, dscores)) * factor
        dqkv_ref[at, cols] = dq.astype(BF16)
        dqkv_ref[at, k_cols] = dk.astype(BF16)
        dqkv_ref[at, v_cols] = dv.astype(BF16)

    @pl.when(second == 1)
    def _():
        for g in range(GROUPS):
            for tile in range(4):
                ds_ref[4 * g + tile, 0, 0:WTOK, :] = (
                    sum_ref[0, 5 * g + tile] + sum_ref[1, 5 * g + tile]
                ).astype(BF16)
            dscore = sum_ref[0, 5 * g + 4] + sum_ref[1, 5 * g + 4]
            for h in range(4):
                pieces = []
                for p in range(3):
                    total = jnp.zeros((8, LANES), F32)
                    for slot in range(8):
                        block = 8 * p + slot
                        if block < ROWBLOCKS:
                            piece = dscore[8 * block : 8 * block + 8, :]
                            turn = (16 * (slot - h)) % LANES
                            if turn:
                                piece = pltpu.roll(piece, turn, 1)
                            total = jnp.where(lane == slot, piece, total)
                    pieces.append(total)
                pieces.append(jnp.zeros((PACKED - USED, LANES), F32))
                ds_ref[4 * g + h, 0, WTOK:PACKED, :] = jnp.concatenate(pieces, axis=0).astype(BF16)

    @pl.when(step == windows - 1)
    def _():
        place_first(ids, near_ref, far_ref, wq_ref)
        rows = unit_ref.shape[0]
        for k in range(rows // LANES):
            sub = slice(LANES * k, LANES * k + LANES)
            turned_ref[:, sub] = unit_ref[sub, :].T
        gain = gain_ref[0:1, 0:width]
        shift = shift_ref[0:1, 0:width]
        gain_sum = jnp.zeros((width, 1), F32)
        shift_sum = jnp.zeros((width, 1), F32)
        for c in range(3):
            sub = slice(width * c, width * c + width)
            values = dqkv_ref[:, sub]
            product = dot_nn(turned_ref[...], values)
            total = jnp.sum(fold8(values.astype(F32)), axis=0, keepdims=True)
            weight = wq_ref[:, sub].astype(F32)
            gain_sum = gain_sum + jnp.sum(product * weight, axis=1, keepdims=True)
            shift_sum = shift_sum + jnp.sum(total * weight, axis=1, keepdims=True)
            column = jnp.broadcast_to(total, (LANES, width)).T[:, 0:1]
            held[sub, :] = (product.T * gain + column * shift).astype(BF16)
        side = mine_ref.shape[0]
        core = ids[0]
        mine_ref[...] = held[ds(core * side, side), :]
        theirs_ref[...] = held[ds((1 - core) * side, side), :]
        small_ref[...] = small_in_ref[...]
        put_rows(small_ref, 0, jnp.broadcast_to(gain_sum, (width, LANES)).T[0:1, :])
        put_rows(small_ref, 6, jnp.broadcast_to(shift_sum, (width, LANES)).T[0:1, :])


def attend_back(ids, qkv, do, p, unit, near, far, gains, shifts, small):
    rows, width = do.shape
    windows = rows // WTOK
    some = windows // 2
    place = lambda i: (i % 2) * some + i // 2
    side = ((3 * width // 2, width), BF16)
    qkv, do, p, unit = far_away(qkv, do, p, unit)
    return launch(
        back_kernel,
        ids,
        (qkv, do, p, unit, near, far, gains, shifts, small),
        [
            pl.BlockSpec((WTOK, 3 * width), lambda i, ids: (place(i), 0)),
            pl.BlockSpec((WTOK, width), lambda i, ids: (place(i), 0)),
            pl.BlockSpec((GROUPS, WTOK, SPAN), lambda i, ids: (place(i), 0, 0)),
        ]
        + wholes((unit, near, far, gains, shifts, small)),
        (
            ((HEADS, some, PACKED, LANES), BF16),
            ((rows, 3 * width), BF16),
            side,
            side,
            ((32, LANES), F32),
        ),
        (
            pl.BlockSpec((HEADS, 1, PACKED, LANES), lambda i, ids: (0, i // 2, 0, 0)),
            whole((rows, 3 * width)),
            whole(side[0]),
            whole(side[0]),
            whole((32, LANES)),
        ),
        [
            pltpu.VMEM((2, 5 * GROUPS, WTOK, LANES), F32),
            pltpu.VMEM((width, 3 * width), BF16),
            pltpu.VMEM((width, rows), BF16),
            pltpu.VMEM((3 * width, width), BF16),
        ],
        16,
        grid=(windows,),
    )


def first_back_kernel(
    ids,
    xn_ref,
    xf_ref,
    dqkv_ref,
    near_ref,
    far_ref,
    dy_ref,
    gain_ref,
    out_ref,
    own_ref,
    send_ref,
    wq_ref,
    dh1_ref,
):
    half, width = xn_ref.shape
    place_first(ids, near_ref, far_ref, wq_ref)
    dh1_ref[...] = dot_nt(dqkv_ref[...], wq_ref[...])
    gain = gain_ref[0:1, 0:width]
    send_ref[0:half, :] = out_ref[...]
    for which, (source, target) in enumerate(((xn_ref, own_ref), (xf_ref, send_ref))):

        def back_block(step, _):
            here = ds(step * WTOK, WTOK)
            at = ds(step * WTOK + which * half, WTOK)
            unit, rstd = norm_stats(source[here, :].astype(F32))
            inner = dh1_ref[at, :] * gain
            first = jnp.mean(inner, axis=-1, keepdims=True)
            second = jnp.mean(inner * unit, axis=-1, keepdims=True)
            dx = dy_ref[at, :].astype(F32) + rstd * (inner - first - unit * second)
            target[at if which else here, :] = dx.astype(BF16)
            return 0

        lax.fori_loop(0, half // WTOK, back_block, 0)


def first_back(ids, tokens, swapped, dqkv, near, far, dy, gains, out_far):
    rows, width = tokens.shape
    tokens, dy, out_far = far_away(tokens, dy, out_far)
    inputs = (tokens, swapped, dqkv, near, far, dy, gains, out_far)
    half = (rows // 2, width)
    return launch(
        first_back_kernel,
        ids,
        inputs,
        [own_half(tokens), half_of(swapped, 0)] + wholes(inputs[2:]),
        ((half, BF16, "hbm"), ((rows, width), BF16, "hbm")),
        (whole(half), whole((rows, width))),
        [pltpu.VMEM((width, 3 * width), BF16), pltpu.VMEM((rows, width), F32)],
        6,
    )


def scatter_kernel(
    ids,
    idx_ref,
    ds_ref,
    small_ref,
    qm_ref,
    qr_ref,
    *refs,
):
    outs = refs[:4]
    both, *sides, acc, table, joined = refs[4:]
    lefts, rights = sides[:2], sides[2:]
    xy = ids[1]
    rows = ds_ref.shape[0]
    highs = lefts[0].shape[0] // rows
    place = lax.broadcasted_iota(I32, (LOW, LANES), 0).astype(F32).astype(BF16)
    one = jnp.ones((LOW, LANES), BF16)
    nothing = jnp.zeros((rows, LANES), BF16)
    acc[...] = jnp.zeros_like(acc)

    def one_block(step, _):
        here = ds(step * 16, 16)
        both[...] = ds_ref[:, here, :].astype(F32).reshape(rows * 16, LANES)
        index = idx_ref[here, :]
        low = (index & (LOW - 1)).astype(F32).astype(BF16)
        high = (index // LOW).astype(F32).astype(BF16)
        product = None
        for part in range(2):
            left, right = lefts[part], rights[part]
            for j in range(8):
                k = 8 * part + j
                cols = slice(LANES * j, LANES * j + LANES)
                right[:, cols] = jnp.where(place == low[k : k + 1, :], one, jnp.zeros_like(one))
                value = both[pl.ds(k, rows, stride=16), :].astype(BF16)
                owner = jnp.broadcast_to(high[k : k + 1, :], (rows, LANES))
                for b in range(highs):
                    left[rows * b : rows * b + rows, cols] = jnp.where(
                        owner == jnp.full((rows, LANES), b, BF16), value, nothing
                    )
            found = dot_nt(left[...], right[...])
            product = found if product is None else product + found
        acc[...] += product
        return 0

    lax.fori_loop(0, idx_ref.shape[0] // 16, one_block, 0)
    table[...] = jnp.zeros_like(table)
    for tile in range(2 * highs):
        t, u = tile // 3, tile % 3
        table[rows * t : rows * t + rows, LANES * u : LANES * u + LANES] = acc[
            rows * (tile // 2) : rows * (tile // 2) + rows,
            LANES * (tile % 2) : LANES * (tile % 2) + LANES,
        ].astype(BF16)
    t, u = 2 * highs // 3, 2 * highs % 3
    table[rows * t : rows * t + 32, LANES * u : LANES * u + LANES] = small_ref[...].astype(BF16)
    joined[0 : qm_ref.shape[0], :] = (
        qm_ref[...].astype(F32) + qr_ref[...].astype(F32)
    ).astype(BF16)
    joined[qm_ref.shape[0] :, :] = table[...]
    shards, piece, _ = outs[0].shape
    for k in range(4):
        for z in range(shards):
            outs[k][z] = joined[ds(((xy ^ k) * shards + z) * piece, piece), :]


def table_gradient(ids, idx, dscores, small, q_mine, q_got, entries, shards):
    rows = dscores.shape[0]
    highs = -(-entries // LOW)
    width = q_mine.shape[1]
    pieces = 4 * shards
    table_rows = rows * (-(-(2 * highs + 1) // 3))
    piece = -(-(q_mine.shape[0] + table_rows) // (16 * pieces)) * 16
    table_rows = pieces * piece - q_mine.shape[0]
    out = ((shards, piece, width), BF16)
    return launch(
        scatter_kernel,
        ids,
        (idx, dscores, small, q_mine, q_got),
        [
            whole(idx.shape),
            whole(dscores.shape),
            whole(small.shape),
            whole(q_mine.shape),
            whole(q_got.shape),
        ],
        (out,) * 4,
        (whole(out[0]),) * 4,
        [
            pltpu.VMEM((rows * 16, LANES), F32),
            pltpu.VMEM((highs * rows, 8 * LANES), BF16),
            pltpu.VMEM((highs * rows, 8 * LANES), BF16),
            pltpu.VMEM((LOW, 8 * LANES), BF16),
            pltpu.VMEM((LOW, 8 * LANES), BF16),
            pltpu.VMEM((highs * rows, LOW), F32),
            pltpu.VMEM((table_rows, width), BF16),
            pltpu.VMEM((pieces * piece, width), BF16),
        ],
        15,
    )


def deal_kernel(count, which, ids, *refs):
    parts, outs, held = refs[:count], refs[count:-1], refs[-1]
    total = parts[0][...].astype(F32)
    for part in parts[1:]:
        total = total + part[...].astype(F32)
    held[...] = total.astype(BF16).reshape(held.shape)
    for k, out in enumerate(outs):
        out[...] = held[ids[which] ^ k]


def deal(ids, which, ways, parts):
    shape = parts[0].shape
    if len(shape) == 2:
        shape = (ways, shape[0] // ways, shape[1])
    out = (shape[1:], BF16)
    return launch(
        functools.partial(deal_kernel, len(parts), which),
        ids,
        parts,
        wholes(parts),
        (out,) * ways,
        (whole(out[0]),) * ways,
        [pltpu.VMEM(shape, BF16)],
        4,
    )


def pass_kernel(ids, a_ref, out_ref):
    out_ref[...] = a_ref[...]


def hand_on(ids, array):
    spec = whole(array.shape)
    return launch(
        pass_kernel, ids, (array,), (spec,), ((array.shape, array.dtype),), (spec,), [], 200
    )[0]


def join_kernel(*refs):
    parts, out = refs[1:-1], refs[-1]
    total = parts[0][...].astype(F32)
    for part in parts[1:]:
        total = total + part[...].astype(F32)
    out[...] = total.astype(BF16)


def join(ids, parts):
    shape = parts[0].shape
    return launch(
        join_kernel, ids, parts, wholes(parts), ((shape, BF16),), (whole(shape),), [], 4
    )[0]


def put_pieces(size, count, place, load):
    for i in range(count):
        start, end = i * size, (i + 1) * size
        while start < end:
            stop, store = place(start, end)
            if store is not None:
                store(load(i, slice(start - i * size, stop - i * size)))
            start = stop


def forward_update_kernel(
    tokens_total,
    ids,
    near_ref,
    far_ref,
    bn_ref,
    bf_ref,
    rn_ref,
    rf_ref,
    r1_ref,
    l1_ref,
    a1_ref,
    m1_ref,
    w1_ref,
    l2_ref,
    a2_ref,
    r2_ref,
    m2_ref,
    w2_ref,
    ap_ref,
    rp_ref,
    lp_ref,
    mp_ref,
    wp_ref,
    r1_out,
    l1_out,
    m1_out,
    w1_out,
    l2_out,
    r2_out,
    m2_out,
    w2_out,
    rp_out,
    lp_out,
    mp_out,
    wp_out,
    g_ref,
    y_ref,
    z_ref,
    lacc_ref,
    racc_ref,
    root_ref,
    turned_ref,
):
    c = pl.program_id(0)
    count = pl.num_programs(0)
    core, xy, s = ids[0], ids[1], ids[2]
    width = g_ref.shape[1]
    ff = count * CHUNK
    piece = l1_ref.shape[0]
    rows = ds(s * piece, piece)
    keep = shampoo_decay
    new = (1.0 - shampoo_decay) / tokens_total
    scale = 1.0 / math.sqrt(tokens_total)

    @pl.when(c == 0)
    def _():
        side = width // 2
        shards = near_ref.shape[1]
        for which, pieces in ((core, near_ref), (1 - core, far_ref)):

            def place(start, end):
                slot = start // side
                stop = min(end, (slot + 1) * side)
                if slot >= g_ref.shape[0]:
                    return end, None
                at = which * side + start - slot * side

                def store(value):
                    g_ref[slot, ds(at, value.shape[0]), :] = value

                return stop, store

            def load(i, rows):
                return pieces[xy ^ (i // shards), s ^ (i % shards), rows, :]

            put_pieces(pieces.shape[2], 4 * shards, place, load)
        half = piece // 2
        for which, ref in ((core, rn_ref), (1 - core, rf_ref)):
            for z in range(shards):
                for i in range(3):
                    root_ref[i, ds(z * piece + which * half, half), :] = ref[
                        z, half * i : half * i + half, :
                    ]
        turned_ref[0] = g_ref[s].T
        turned_ref[1] = g_ref[count + s].T
        for i in range(y_ref.shape[0]):
            y_ref[i] = dot_nn(a1_ref[...].astype(BF16), g_ref[i]).astype(BF16)
        z_ref[...] = jnp.zeros_like(z_ref)
        lacc_ref[...] = jnp.zeros_like(lacc_ref)
        racc_ref[...] = jnp.zeros_like(racc_ref)

    g1 = g_ref[c]
    g2 = g_ref[count + c]
    r1_out[...] = keep * r1_ref[...] + (new / width) * dot_nn(turned_ref[0], g1)
    l2_out[...] = keep * l2_ref[...] + (new / width) * dot_nn(turned_ref[1], g2)
    shards = bn_ref.shape[0]
    steps = count // 2

    def first_columns(which, ref):
        change = dot_nn(y_ref[0], ref[0])
        for z in range(1, shards):
            change = change + dot_nn(y_ref[z], ref[z])
        cols = pl.ds(
            pl.multiple_of(which * (ff // 2) + c % steps * CHUNK, LANES), CHUNK
        )
        momentum = shampoo_momentum * m1_ref[:, cols] + change * scale
        m1_out[:, cols] = momentum
        w1_out[:, cols] = w1_ref[:, cols] - matrix_rates[2] * momentum

    @pl.when(c < steps)
    def _():
        first_columns(core, bn_ref)

    @pl.when(c >= steps)
    def _():
        first_columns(1 - core, bf_ref)

    z_ref[...] += dot_nt(a2_ref[...].astype(BF16), g2)
    lacc_ref[...] += dot_nt(g_ref[c, rows, :], g1)
    racc_ref[...] += dot_nt(g_ref[count + c, rows, :], g2)

    @pl.when(c == count - 1)
    def _():
        l1_out[...] = keep * l1_ref[...] + (new / ff) * lacc_ref[...]
        r2_out[...] = keep * r2_ref[...] + (new / ff) * racc_ref[...]
        change = dot_nn(z_ref[...].astype(BF16), root_ref[2]) * scale
        momentum = shampoo_momentum * m2_ref[...] + change
        m2_out[...] = momentum
        w2_out[...] = w2_ref[...] - matrix_rates[3] * momentum
        gp = g_ref[2 * count]
        z_ref[...] = dot_tn(gp, gp)
        rp_out[...] = keep * rp_ref[...] + (new / width) * z_ref[rows, :]
        lp_out[...] = keep * lp_ref[...] + (new / width) * dot_nt(g_ref[2 * count, rows, :], gp)
        first = dot_nn(ap_ref[...].astype(BF16), gp).astype(BF16)
        change = dot_nn(first, root_ref[0]) * scale
        momentum = shampoo_momentum * mp_ref[...] + change
        mp_out[...] = momentum
        wp_out[...] = wp_ref[...] - matrix_rates[1] * momentum


def forward_update(
    total, ids, near, far, r_near, r_far, r1, l1, a1, m1, w1, l2, a2, r2, m2, w2, ap, rp, lp, mp, wp
):
    shards, width = near.shape[1], near.shape[3]
    count = r1.shape[1] // CHUNK
    steps = count // 2
    rank_rows = r1.shape[0]
    piece = l1.shape[0]
    assert rank_rows == CHUNK == width
    column = pl.BlockSpec((rank_rows, CHUNK), lambda c, ids: (0, c))
    updated = (r1, l1, m1, w1, l2, r2, m2, w2, rp, lp, mp, wp)
    (r_near,) = far_away(r_near)
    inputs = (
        near,
        far,
        r_near,
        r_far,
        r_near,
        r_far,
        *far_away(r1, l1, a1, m1, w1, l2, a2, r2, m2, w2, ap, rp, lp, mp, wp),
    )
    block = (shards, rank_rows, width)
    rest = (shards, rank_rows // 2, width)
    place = lambda c, ids: (0, 2 * steps, 0)
    roots = [
        pl.BlockSpec(block, lambda c, ids: (0, jnp.minimum(c, steps - 1), 0)),
        pl.BlockSpec(block, lambda c, ids: (0, jnp.maximum(c - steps, 0), 0)),
        pl.BlockSpec(rest, place),
        pl.BlockSpec(rest, place),
    ]
    return launch(
        functools.partial(forward_update_kernel, total),
        ids,
        inputs,
        wholes(inputs[:2])
        + roots
        + [column if i in (6, 11, 12) else whole(inputs[i].shape) for i in range(6, len(inputs))],
        [(a.shape, F32) for a in updated],
        [column if i in (0, 4) else whole(a.shape) for i, a in enumerate(updated)],
        [
            pltpu.VMEM((2 * count + 1, width, CHUNK), BF16),
            pltpu.VMEM((count, piece, CHUNK), BF16),
            pltpu.VMEM((rank_rows, width), F32),
            pltpu.VMEM(l1.shape, F32),
            pltpu.VMEM(r2.shape, F32),
            pltpu.VMEM((3, width, width), BF16),
            pltpu.VMEM((2, width, width), BF16),
        ],
        12,
        grid=(count,),
        limit=40,
    )


def attention_update_kernel(
    tokens_total,
    ids,
    near_ref,
    far_ref,
    rn_ref,
    rf_ref,
    aq_ref,
    rq_ref,
    lq_ref,
    mq_ref,
    wq_ref,
    rq_out,
    lq_out,
    mq_out,
    wq_out,
    square,
    g_ref,
    root_ref,
):
    core, xy, s = ids[0], ids[1], ids[2]
    piece, width = lq_ref.shape
    span = rq_ref.shape[0]
    full_width = rq_ref.shape[1]
    side = full_width // 2
    shards = near_ref.shape[1]
    for which, pieces in ((core, near_ref), (1 - core, far_ref)):

        def place(start, end):
            if start >= side:
                return end, None

            def store(value):
                g_ref[ds(which * side + start, value.shape[0]), :] = value

            return min(end, side), store

        def load(i, rows):
            return pieces[xy ^ (i // shards), s ^ (i % shards), rows, :]

        put_pieces(pieces.shape[2], 4 * shards, place, load)

    part = span // 2
    for which, ref in ((core, rn_ref), (1 - core, rf_ref)):
        for z in range(shards):
            for c in range(full_width // width):
                at = ref.shape[1] - part * (full_width // width - c)
                root_ref[ds(z * span + which * part, part), width * c : width * c + width] = ref[
                    z, at : at + part, :
                ]
    rows = ds(s * piece, piece)
    some = ds(s * span, span)
    keep = shampoo_decay
    new = (1.0 - shampoo_decay) / tokens_total
    gq = g_ref[...]
    rq_out[...] = keep * rq_ref[...] + (new / width) * dot_nt(g_ref[some, :], gq)
    square[...] = dot_tn(gq, gq)
    lq_out[...] = keep * lq_ref[...] + (new / full_width) * square[rows, :]
    first = dot_nt(aq_ref[...].astype(BF16), gq).astype(BF16)
    change = dot_nn(first, root_ref[...]) * (1.0 / math.sqrt(tokens_total))
    momentum = shampoo_momentum * mq_ref[...] + change
    mq_out[...] = momentum
    wq_out[...] = wq_ref[...] - matrix_rates[0] * momentum


def attention_update(total, ids, near, far, r_near, r_far, aq, rq, lq, mq, wq):
    shards, width = near.shape[1], near.shape[3]
    (r_near,) = far_away(r_near)
    inputs = (near, far, r_near, r_far, *far_away(aq, rq, lq, mq, wq))
    some = pl.BlockSpec((shards, r_near.shape[1] // 2, width), lambda i, ids: (0, 1, 0))
    updated = (rq, lq, mq, wq)
    return launch(
        functools.partial(attention_update_kernel, total),
        ids,
        inputs,
        wholes(inputs[:2]) + [some, some] + wholes(inputs[4:]),
        [(a.shape, F32) for a in updated],
        wholes(updated),
        [
            pltpu.VMEM((width, width), F32),
            pltpu.VMEM((rq.shape[1], width), BF16),
            pltpu.VMEM((rq.shape[1], rq.shape[1]), BF16),
        ],
        3,
    )


def adam_update(parameter, first_moment, second_moment, gradient):
    new_first = adam_first * first_moment + (1.0 - adam_first) * gradient
    new_second = adam_second * second_moment + (1.0 - adam_second) * gradient * gradient
    first_hat = new_first / (1.0 - adam_first**STEP)
    second_hat = new_second / (1.0 - adam_second**STEP)
    return (
        parameter - adam_rate * first_hat / (jnp.sqrt(second_hat) + adam_eps),
        new_first,
        new_second,
    )


def table_kernel(
    tokens_total,
    skip,
    ids,
    near_ref,
    far_ref,
    t_ref,
    f_ref,
    q_ref,
    on_ref,
    in_ref,
    got_ref,
    t_out,
    f_out,
    q_out,
    v_out,
    block_ref,
    grad_ref,
    held,
    turned,
):
    core, xy, s = ids[0], ids[1], ids[2]
    heads, kinds, entries = t_ref.shape
    scale = 1.0 / math.sqrt(tokens_total)
    shards, size = near_ref.shape[1], near_ref.shape[2]
    some = kinds // 2
    width = held.shape[2]
    tiles = -(-entries // LANES)
    total = some * HEADS

    @pl.when(pl.program_id(0) == 0)
    def _():
        for i in range(skip // size, 4 * shards):
            start = i * size - skip
            for which, pieces in ((core, near_ref), (1 - core, far_ref)):
                held[which, start : start + size, :] = (
                    pieces[xy ^ (i // shards), s ^ (i % shards)].astype(F32) * scale
                )
        for h in range(HEADS):
            for u in range(turned.shape[2] // width):
                at = slice(total * u + some * h, total * u + some * h + some)
                cols = slice(width * u, width * u + width)
                turned[h, 0:some, cols] = held[0, at, :]
                turned[h, some:kinds, cols] = held[1, at, :]
        per = width // LANES
        start, at = total * (tiles // per), LANES * (tiles % per)
        v_out[...] = (
            held[0, start : start + 32, at : at + LANES]
            + held[1, start : start + 32, at : at + LANES]
        )
        half = on_ref.shape[0]
        for own, ref, at in ((on_ref, block_ref, 0), (in_ref, grad_ref, half)):
            ref[ds(core * half, half), :] = own[...]
            ref[ds((1 - core) * half, half), :] = got_ref[at : at + half, :]

    first = pl.program_id(0) * heads
    for h in range(heads):
        grad = turned[first + h, :, 0:entries]
        t_out[h], f_out[h], q_out[h] = adam_update(t_ref[h], f_ref[h], q_ref[h], grad)


def table_update(total, ids, near, far, skip, table, first, second, out_own, in_own, got):
    shards, piece, width = near.shape[1:]
    heads, kinds, entries = table.shape
    assert skip % piece == 0
    block = pl.BlockSpec((heads // 4, kinds, entries), lambda i, ids: (i, 0, 0))
    out_own, in_own, got = far_away(out_own, in_own, got)
    inputs = (near, far, *far_away(table, first, second), out_own, in_own, got)
    outputs = ((table.shape, F32),) * 3 + (((32, LANES), F32),) + ((got.shape, BF16),) * 2
    return launch(
        functools.partial(table_kernel, total, skip),
        ids,
        inputs,
        wholes(inputs[:2]) + [block] * 3 + wholes(inputs[5:]),
        outputs,
        [block] * 3 + [whole(o[0]) for o in outputs[3:]],
        [
            pltpu.VMEM((2, 4 * shards * piece - skip, width), F32),
            pltpu.VMEM((heads, kinds, -(-entries // width) * width), F32),
        ],
        3,
        grid=(4,),
    )


XY = ("y", "x")


def swap(array, axes, k, size):
    return lax.ppermute(array, axes, [(i, i ^ k) for i in range(size)])


def after(array, *others):
    return lax.optimization_barrier((array, *others))[0]


def per_device(
    tokens,
    cotangent,
    rel_index,
    qkv_weight,
    proj_weight,
    fc1_weight,
    fc2_weight,
    qkv_momentum,
    proj_momentum,
    fc1_momentum,
    fc2_momentum,
    qkv_left,
    qkv_right,
    proj_left,
    proj_right,
    fc1_left,
    fc1_right,
    fc2_left,
    fc2_right,
    qkv_left_root,
    qkv_right_root,
    proj_left_root,
    proj_right_root,
    fc1_left_root,
    fc1_right_root,
    fc2_left_root,
    fc2_right_root,
    norm_gains,
    biases,
    bias_table,
    gains_first,
    gains_second,
    biases_first,
    biases_second,
    table_first,
    table_second,
):
    shards = lax.axis_size("fsdp")
    outer = lax.axis_size("outer")
    core = lax.axis_index("core")
    z = lax.axis_index("fsdp")
    xy = lax.axis_index("y") * 2 + lax.axis_index("x")
    ids = jnp.stack([core, xy, z]).astype(I32)
    rows, width = tokens.shape
    total = rows * outer * 8 * shards
    kinds, heads, entries = bias_table.shape
    assert rows // WTOK == kinds and heads == HEADS and shards == 4
    ff = fc1_weight.shape[1]

    pieces = 4 * shards

    def scatter_xy(parts, *before):
        parts = [parts[0]] + [swap(parts[k], XY, k, 4) for k in range(1, 4)]
        return deal(after(ids, *before), 2, shards, parts)

    def scatter_z(parts, *before):
        parts = [parts[0]] + [swap(parts[k], "fsdp", k, shards) for k in range(1, shards)]
        piece = join(after(ids, *before), parts)
        return lax.psum(piece, "outer") if outer > 1 else piece

    def gather_z(piece):
        return jnp.stack([piece] + [swap(piece, "fsdp", k, shards) for k in range(1, shards)])

    def gather_xy(piece, *before):
        pieces = [piece] + [swap(piece, XY, k, 4) for k in range(1, 4)]
        return jnp.stack([after(pieces[0], *before)] + pieces[1:])

    table_of = lambda array: array.transpose(1, 0, 2)
    table, table_f, table_q = map(table_of, (bias_table, table_first, table_second))

    first, others_own, swapped = pack(
        ids, tokens, cotangent, qkv_weight, proj_weight, fc1_weight, fc2_weight
    )
    swapped = swap(swapped, "core", 1, 2)
    roots_own = pack_roots(
        after(ids, first),
        proj_right_root,
        fc1_left_root,
        fc2_right_root,
        qkv_right_root,
        fc1_right_root,
    )
    others = lax.all_gather(others_own, "fsdp", axis=0)

    gains = norm_gains.reshape(1, -1)
    shifts = biases.reshape(1, -1)
    bias, idx = bias_gather(after(ids, first, roots_own), rel_index, table)
    first_near = [swap(first, "fsdp", k, shards) for k in range(1, shards)]
    first_near = jnp.stack([after(first, bias)] + first_near)
    first_far = swap(first_near, "core", 1, 2)
    qkv, unit, p, mixed = attend(
        ids, tokens, swapped, first_near, first_far, gains, shifts, bias
    )
    others_far = swap(after(others, mixed), "core", 1, 2)
    roots = lax.all_gather(after(roots_own, mixed), "fsdp", axis=0)
    out_own, out_far, dy, do, g_mine, g_theirs, small = middle(
        ids, tokens, swapped, mixed, cotangent, others, others_far, gains, shifts, ff, pieces
    )
    g_got = swap(g_theirs, "core", 1, 2)
    small = hand_on(ids, small)
    g_parts = deal(after(ids, small), 1, 4, (g_mine, g_got))
    g_parts = [part.reshape(shards, -1, width) for part in g_parts]
    dscores, dqkv, q_mine, q_theirs, small = attend_back(
        after(ids, *g_parts), qkv, do, p, unit, first_near, first_far, gains, shifts, small
    )
    q_got = swap(q_theirs, "core", 1, 2)
    g_parts = scatter_xy(g_parts, q_mine)
    parts = table_gradient(
        after(ids, *g_parts),
        idx,
        dscores.reshape(-1, PACKED, LANES),
        small,
        q_mine,
        q_got,
        entries,
        shards,
    )
    g_piece = scatter_z(g_parts, parts[0])
    in_own, in_far = first_back(
        after(ids, g_piece), tokens, swapped, dqkv, first_near, first_far, dy, gains, out_far
    )
    parts = scatter_xy(parts, in_far)
    got = swap(in_far, "core", 1, 2)
    g_piece = gather_z(g_piece)
    piece = scatter_z(parts, g_piece)
    g_near = gather_xy(g_piece, piece)
    piece = gather_z(piece)
    near = gather_xy(piece, g_near)
    far = swap(near, "core", 1, 2)
    roots_far = swap(after(roots, far, got), "core", 1, 2)
    g_far = swap(after(g_near, far, got), "core", 1, 2)
    *table_out, vectors, block_output, input_grad = table_update(
        total,
        after(ids, near),
        near,
        far,
        3 * width // 2,
        table,
        table_f,
        table_q,
        out_own,
        in_own,
        got,
    )
    rq, lq, mq, wq = attention_update(
        total,
        ids,
        near,
        far,
        roots,
        roots_far,
        qkv_left_root,
        qkv_right,
        qkv_left,
        qkv_momentum,
        qkv_weight,
    )
    r1, l1, m1, w1, l2, r2, m2, w2, rp, lp, mp, wp = forward_update(
        total,
        after(ids, rq),
        g_near,
        g_far,
        roots,
        roots_far,
        fc1_right,
        fc1_left,
        fc1_left_root,
        fc1_momentum,
        fc1_weight,
        fc2_left,
        fc2_left_root,
        fc2_right,
        fc2_momentum,
        fc2_weight,
        proj_left_root,
        proj_right,
        proj_left,
        proj_momentum,
        proj_weight,
    )
    table_out = [table_of(array) for array in table_out]
    vectors = vectors.reshape(-1)
    size = norm_gains.shape[0]
    gains_out = adam_update(norm_gains, gains_first, gains_second, vectors[:size])
    biases_out = adam_update(
        biases, biases_first, biases_second, vectors[size : size + biases.shape[0]]
    )
    return (
        block_output,
        input_grad,
        wq,
        wp,
        w1,
        w2,
        mq,
        mp,
        m1,
        m2,
        lq,
        rq,
        lp,
        rp,
        l1,
        r1,
        l2,
        r2,
        gains_out[0],
        biases_out[0],
        table_out[0],
        gains_out[1],
        biases_out[1],
        table_out[1],
        gains_out[2],
        biases_out[2],
        table_out[2],
    )


def solution(mesh):
    dp, fsdp = mesh.devices.shape
    split_mesh = jax.sharding.Mesh(
        mesh.devices.reshape(dp // 8, 2, 2, 2, fsdp), ("outer", "y", "x", "core", "fsdp")
    )
    rows = P(("outer", "y", "x", "core", "fsdp"), None)
    shard = P("fsdp", None)
    return jax.shard_map(
        per_device,
        mesh=split_mesh,
        in_specs=(rows, rows) + (P(),) + (shard,) * 24 + (P(),) * 9,
        out_specs=(rows, rows) + (shard,) * 16 + (P(),) * 9,
        check_vma=False,
    )
```
